32 devices in a mesh: dp: 4 (over z), ctx: 8 (over y, x, core).
Axes of the slice: x: 2, y: 2, z: 4, core: 2. Of those that a mesh axis runs over, the one named last changes fastest.
Arguments:
- inputs: bfloat16 [4, 4096, 1536], P(None, ('dp', 'ctx')), may hold values from -6 to 6
- doc_ids: int32 [4, 4096], P(None, ('dp', 'ctx')), may hold values from 1 to 3, as said below
- cotangent: bfloat16 [4, 4096, 1536], P(None, ('dp', 'ctx')), may hold values from -6 to 6
- attend_in: float32 [1536, 3072], P(('dp', 'ctx')), may hold values from -0.15625 to 0.15625
- attend_out: float32 [1536, 1536], P(('dp', 'ctx')), may hold values from -1.75 to 1.75
- gains: float32 [2, 1536], P(None, ('dp', 'ctx')), may hold values from 0.5 to 1.5
- expand: float32 [1536, 8192], P(('dp', 'ctx')), may hold values from -0.15625 to 0.15625
- contract: float32 [4096, 1536], P(('dp', 'ctx')), may hold values from -0.09375 to 0.09375
- attend_in_first: float32 [1536, 3072], P(('dp', 'ctx'))
- attend_in_second: float32 [1536, 3072], P(('dp', 'ctx')), as said below
- attend_out_first: float32 [1536, 1536], P(('dp', 'ctx'))
- attend_out_second: float32 [1536, 1536], P(('dp', 'ctx')), as said below
- gains_first: float32 [2, 1536], P(None, ('dp', 'ctx'))
- gains_second: float32 [2, 1536], P(None, ('dp', 'ctx')), as said below
- expand_first: float32 [1536, 8192], P(('dp', 'ctx'))
- expand_second: float32 [1536, 8192], P(('dp', 'ctx')), as said below
- contract_first: float32 [4096, 1536], P(('dp', 'ctx'))
- contract_second: float32 [4096, 1536], P(('dp', 'ctx')), as said below
Outputs:
- block_out: bfloat16 [4, 4096, 1536], P(None, ('dp', 'ctx'))
- grad_inputs: bfloat16 [4, 4096, 1536], P(None, ('dp', 'ctx'))
- new_attend_in: float32 [1536, 3072], P(('dp', 'ctx'))
- new_attend_in_first: float32 [1536, 3072], P(('dp', 'ctx'))
- new_attend_in_second: float32 [1536, 3072], P(('dp', 'ctx'))
- new_attend_out: float32 [1536, 1536], P(('dp', 'ctx'))
- new_attend_out_first: float32 [1536, 1536], P(('dp', 'ctx'))
- new_attend_out_second: float32 [1536, 1536], P(('dp', 'ctx'))
- new_gains: float32 [2, 1536], P(None, ('dp', 'ctx'))
- new_gains_first: float32 [2, 1536], P(None, ('dp', 'ctx'))
- new_gains_second: float32 [2, 1536], P(None, ('dp', 'ctx'))
- new_expand: float32 [1536, 8192], P(('dp', 'ctx'))
- new_expand_first: float32 [1536, 8192], P(('dp', 'ctx'))
- new_expand_second: float32 [1536, 8192], P(('dp', 'ctx'))
- new_contract: float32 [4096, 1536], P(('dp', 'ctx'))
- new_contract_first: float32 [4096, 1536], P(('dp', 'ctx'))
- new_contract_second: float32 [4096, 1536], P(('dp', 'ctx'))
The draws below stay inside these ranges and needn't reach their ends.
Inputs may be any that keep to these rules, and one draw needn't show every extreme that they name: `doc_ids`: each row is 4 streams of 1024 tokens end to end. Within a stream the ids never fall and begin at 1. At each stream place, one of the 4 rows holds a single document that fills the whole stream; the other streams end at id 3. `attend_in_second`: positive. `attend_out_second`: positive. `gains_second`: positive. `expand_second`: positive. `contract_second`: positive.
All inputs are finite; a program needn't handle non-finite values.
Results may differ from the reference program's by a relative error of at most 0.019.
Values may be sent and summed in bfloat16 or wider, within the bound.
No kernel may reach another device: no remote copies, remote signals or barrier semaphores. Data moves between devices by JAX's collectives and lax.ppermute only.
A program may use at most 384 MiB of HBM per device.

```python
import math
import jax
import jax.numpy as jnp
from jax import lax

D = 1536
HEADS = 16
KV_HEADS = 8
HEAD_DIM = 96
FF = 4096
MB = 4
NDOC = 3
STEP = 10
TOK_MB = 128
JOINED = 3072
STREAM = 1024
TOKENS = 4096
N_DP = 4
N_CTX = 8


def grad_size(factor):
    return factor * math.sqrt(MB * TOKENS)


def first_moment(key, shape, factor):
    return 0.1 / 0.9 * grad_size(factor) * jax.random.normal(key, shape, jnp.float32)


def second_moment(key, shape, factor):
    spread = jnp.exp(jax.random.uniform(key, shape, jnp.float32, math.log(0.5), math.log(8.0)))
    return 0.05 / 0.95 * grad_size(factor) ** 2 * spread


def draw_doc_ids(key, part):
    key = jax.random.fold_in(key, 7)
    stream = N_CTX * TOK_MB
    pick_key, cut_key = jax.random.split(key)
    single = jax.random.randint(pick_key, (N_DP, 1), 0, MB)
    cuts = jax.random.randint(cut_key, (N_DP, MB, NDOC - 1), 1, stream)
    places = jnp.arange(stream, dtype=jnp.int32)
    counted = jnp.sum((cuts[:, :, None, :] <= places[None, None, :, None]).astype(jnp.int32), axis=-1)
    whole = (jnp.arange(MB, dtype=jnp.int32)[None, :] == single)[:, :, None]
    ident = jnp.where(whole, 1, 1 + counted)
    return jnp.transpose(ident, (1, 0, 2)).reshape(MB, N_DP * stream).astype(jnp.int32)


def draw_attend_in_first(key, part):
    key = jax.random.fold_in(key, 21)
    return first_moment(key, (D, JOINED), 0.3)


def draw_attend_in_second(key, part):
    key = jax.random.fold_in(key, 22)
    return second_moment(key, (D, JOINED), 0.3)


def draw_attend_out_first(key, part):
    key = jax.random.fold_in(key, 23)
    return first_moment(key, (HEADS * HEAD_DIM, D), 0.1)


def draw_attend_out_second(key, part):
    key = jax.random.fold_in(key, 24)
    return second_moment(key, (HEADS * HEAD_DIM, D), 0.1)


def draw_gains_first(key, part):
    key = jax.random.fold_in(key, 25)
    return first_moment(key, (2, D), 0.5)


def draw_gains_second(key, part):
    key = jax.random.fold_in(key, 26)
    return second_moment(key, (2, D), 0.5)


def draw_expand_first(key, part):
    key = jax.random.fold_in(key, 27)
    return first_moment(key, (D, 2 * FF), 0.4)


def draw_expand_second(key, part):
    key = jax.random.fold_in(key, 28)
    return second_moment(key, (D, 2 * FF), 0.4)


def draw_contract_first(key, part):
    key = jax.random.fold_in(key, 29)
    return first_moment(key, (FF, D), 0.5)


def draw_contract_second(key, part):
    key = jax.random.fold_in(key, 30)
    return second_moment(key, (FF, D), 0.5)


def levels(stream_key, extent, shards, low, high):
    factor_of = 1.0
    for dim, shards_of in shards:
        steps = jax.random.uniform(jax.random.fold_in(jax.random.fold_in(stream_key, 6), dim), (shards_of,), jnp.float32, low / len(shards), high / len(shards))
        factor_of = factor_of * jnp.repeat(jnp.exp(steps), extent[dim] // shards_of).reshape((-1,) + (1,) * (len(extent) - 1 - dim))
    return factor_of


def gaussian(key, dims, scale, bound, pieces=(), kind=jnp.bfloat16):
    gain = levels(key, dims, pieces, -0.22, 0.18) if pieces else 1.0
    values = jax.random.normal(key, dims, jnp.float32) * scale * gain
    return jnp.minimum(jnp.maximum(values, -bound), bound).astype(kind)


def setup_inputs(seed: int = 0) -> dict:
    streams_of = jax.random.split(jax.random.key(seed), 19)
    return {
        "inputs": gaussian(streams_of[0], (MB, TOKENS, D), 1.0, 6.0, ((1, 32),)),
        "doc_ids": draw_doc_ids(jax.random.fold_in(streams_of[18], 71), 0),
        "cotangent": gaussian(streams_of[2], (MB, TOKENS, D), 1.0, 6.0, ((1, 32),)),
        "attend_in": gaussian(streams_of[3], (D, JOINED), D ** -0.5, 0.15625, ((0, 32),), jnp.float32),
        "attend_out": gaussian(streams_of[4], (HEADS * HEAD_DIM, D), (max(1, (HEADS * HEAD_DIM) // (STREAM // 8))) ** -0.5, 1.75, ((0, 32),), jnp.float32),
        "gains": jnp.clip(1.0 + 0.1 * jax.random.normal(streams_of[5], (2, D), jnp.float32), 0.5, 1.5),
        "expand": gaussian(streams_of[6], (D, 2 * FF), D ** -0.5, 0.15625, ((0, 32),), jnp.float32),
        "contract": gaussian(streams_of[7], (FF, D), FF ** -0.5, 0.09375, ((0, 32),), jnp.float32),
        "attend_in_first": draw_attend_in_first(jax.random.fold_in(streams_of[18], 71), 0),
        "attend_in_second": draw_attend_in_second(jax.random.fold_in(streams_of[18], 71), 0),
        "attend_out_first": draw_attend_out_first(jax.random.fold_in(streams_of[18], 71), 0),
        "attend_out_second": draw_attend_out_second(jax.random.fold_in(streams_of[18], 71), 0),
        "gains_first": draw_gains_first(jax.random.fold_in(streams_of[18], 71), 0),
        "gains_second": draw_gains_second(jax.random.fold_in(streams_of[18], 71), 0),
        "expand_first": draw_expand_first(jax.random.fold_in(streams_of[18], 71), 0),
        "expand_second": draw_expand_second(jax.random.fold_in(streams_of[18], 71), 0),
        "contract_first": draw_contract_first(jax.random.fold_in(streams_of[18], 71), 0),
        "contract_second": draw_contract_second(jax.random.fold_in(streams_of[18], 71), 0),
    }


EPSILON = 1e-06
ROPE_BASE = 100000.0
BETA_ONE = 0.9
BETA_TWO = 0.95
ADAM_EPSILON = 1e-08
DECAY = 0.1
RATE = 0.3
GAIN_RATE = 0.25

@jax.custom_vjp
def low(v):
    return lax.optimization_barrier(v.astype(jnp.bfloat16)).astype(jnp.float32)

@jax.custom_vjp
def low_back(v):
    return v

def low_keep(v):
    return (low(v), None)

def low_pass(kept, grad):
    return (grad,)

def back_keep(v):
    return (v, None)

def back_low(kept, grad):
    return (low(grad),)
low.defvjp(low_keep, low_pass)
low_back.defvjp(back_keep, back_low)

def matmul(left, right):
    return jnp.dot(left, right, precision=lax.Precision.HIGHEST, preferred_element_type=jnp.float32)

def rotate(values, cosine, sine):
    half = values.shape[-1] // 2
    first, second = (values[..., :half], values[..., half:])
    return jnp.concatenate([first * cosine - second * sine, second * cosine + first * sine], axis=-1)

def attention(query, keys, values, ident):
    length = query.shape[0]
    groups = HEADS // KV_HEADS
    query4 = query.reshape(length, KV_HEADS, groups, HEAD_DIM)
    logits = jnp.einsum('qkgd,ckd->kgqc', query4, keys, precision=lax.Precision.HIGHEST)
    logits = low_back(logits * HEAD_DIM ** (-0.5))
    places = jnp.arange(length, dtype=jnp.int32)
    mask = (ident[:, None] == ident[None, :]) & (places[:, None] >= places[None, :])
    masked = jnp.where(mask, logits, -1e+30)
    peak = lax.optimization_barrier(jnp.max(masked, axis=-1, keepdims=True))
    expo = jnp.where(mask, jnp.exp(masked - peak), 0.0)
    weights = expo / lax.optimization_barrier(jnp.sum(expo, axis=-1, keepdims=True))
    attended = jnp.einsum('kgqc,ckd->qkgd', weights, values, precision=lax.Precision.HIGHEST)
    return attended.reshape(length, HEADS * HEAD_DIM)

def forward(resid, ident, attend_in, attend_out, gains, expand, contract):
    length = resid.shape[0]
    w_in = low(attend_in)
    w_out = low(attend_out)
    gain_low = low(gains)
    w_expand = low(expand)
    w_contract = low(contract)
    places = jnp.arange(length, dtype=jnp.int32)
    before = lax.optimization_barrier(jnp.sum((ident[None, :] < ident[:, None]).astype(jnp.int32), axis=1))
    position = (places - before).astype(jnp.float32)
    half = HEAD_DIM // 2
    inverse = jnp.power(ROPE_BASE, -2.0 * jnp.arange(half, dtype=jnp.float32) / HEAD_DIM)
    angles = position[:, None, None] * inverse
    cosine = jnp.cos(angles)
    sine = jnp.sin(angles)
    inv_one = lax.rsqrt(lax.optimization_barrier(jnp.mean(resid * resid, axis=-1, keepdims=True)) + EPSILON)
    first_in = low(resid * inv_one * gain_low[0])
    joined = low_back(matmul(first_in, w_in))
    qwidth = HEADS * HEAD_DIM
    kwidth = KV_HEADS * HEAD_DIM
    query = low(rotate(joined[:, :qwidth].reshape(length, HEADS, HEAD_DIM), cosine, sine))
    keys = low(rotate(joined[:, qwidth:qwidth + kwidth].reshape(length, KV_HEADS, HEAD_DIM), cosine, sine))
    values = low(joined[:, qwidth + kwidth:].reshape(length, KV_HEADS, HEAD_DIM))
    attended = low_back(low(jax.checkpoint(attention)(query, keys, values, ident)))
    hidden_res = resid + low_back(matmul(attended, w_out))
    inv_two = lax.rsqrt(lax.optimization_barrier(jnp.mean(hidden_res * hidden_res, axis=-1, keepdims=True)) + EPSILON)
    second_in = low(hidden_res * inv_two * gain_low[1])
    gate_up = low_back(matmul(second_in, w_expand))
    gate = gate_up[:, :FF]
    upward = gate_up[:, FF:]
    mixed = low(gate * jax.nn.sigmoid(gate) * upward)
    return hidden_res + low_back(matmul(mixed, w_contract))

def adamw(weight, first, second, grad, rate):
    first_new = BETA_ONE * first + (1.0 - BETA_ONE) * grad
    second_new = BETA_TWO * second + (1.0 - BETA_TWO) * grad * grad
    ratio = first_new / (1.0 - BETA_ONE ** STEP) / (jnp.sqrt(second_new / (1.0 - BETA_TWO ** STEP)) + ADAM_EPSILON)
    return (weight - rate * (ratio + DECAY * weight), first_new, second_new)

def reference(inputs, doc_ids, cotangent, attend_in, attend_out, gains, expand, contract, attend_in_first, attend_in_second, attend_out_first, attend_out_second, gains_first, gains_second, expand_first, expand_second, contract_first, contract_second):
    streams = MB * N_DP
    resid_all = inputs.astype(jnp.float32).reshape(streams, STREAM, D)
    ident_all = doc_ids.reshape(streams, STREAM).astype(jnp.int32)
    cot_all = cotangent.astype(jnp.float32).reshape(streams, STREAM, D)
    params = (attend_in, attend_out, gains, expand, contract)

    def one_stream(accum, items):
        resid, ident, cot = items

        def apply(value, w_in, w_out, gain_all, w_expand, w_contract):
            return forward(value, ident, w_in, w_out, gain_all, w_expand, w_contract)
        result, pull = jax.vjp(apply, resid, *params)
        grads = pull(cot)
        accum = tuple((total + piece for total, piece in zip(accum, grads[1:])))
        return (accum, (result.astype(jnp.bfloat16), grads[0].astype(jnp.bfloat16)))
    start = tuple((jnp.zeros_like(weight) for weight in params))
    sums, (outputs, input_grads) = lax.scan(one_stream, start, (resid_all, ident_all, cot_all))
    block_out = outputs.reshape(MB, TOKENS, D)
    grad_inputs = input_grads.reshape(MB, TOKENS, D)
    out_fan = max(1, HEADS * HEAD_DIM // (STREAM // 8))
    new_in = adamw(attend_in, attend_in_first, attend_in_second, sums[0], RATE / math.sqrt(D))
    new_out = adamw(attend_out, attend_out_first, attend_out_second, sums[1], RATE / math.sqrt(out_fan))
    new_gain = adamw(gains, gains_first, gains_second, sums[2], GAIN_RATE)
    new_expand = adamw(expand, expand_first, expand_second, sums[3], RATE / math.sqrt(D))
    new_contract = adamw(contract, contract_first, contract_second, sums[4], RATE / math.sqrt(FF))
    return (block_out, grad_inputs, new_in[0], new_in[1], new_in[2], new_out[0], new_out[1], new_out[2], new_gain[0], new_gain[1], new_gain[2], new_expand[0], new_expand[1], new_expand[2], new_contract[0], new_contract[1], new_contract[2])
```

```python
import functools
import math

import jax
import jax.numpy as jnp
import numpy as np
from jax import lax
from jax.experimental import pallas as pl
from jax.experimental.pallas import tpu as pltpu
from jax.sharding import PartitionSpec as P

D = 1536
HEADS = 16
KV_HEADS = 8
HEAD_DIM = 96
FF = 4096
STEP = 10

EPSILON = 1e-06
ROPE_BASE = 100000.0
BETA_ONE = 0.9
BETA_TWO = 0.95
ADAM_EPSILON = 1e-08
DECAY = 0.1
RATE = 0.3
GAIN_RATE = 0.25

HALF = HEAD_DIM // 2
SLOT = 128
SCALING = HEAD_DIM ** (-0.5)
LOG2E = math.log2(math.e)
VMEM_LIMIT = 60 * 1024 * 1024
BF16 = jnp.bfloat16
F32 = jnp.float32
SMALL_COST = pl.CostEstimate(flops=1 << 20, bytes_accessed=1 << 20, transcendentals=0)


def against(left, right):
    return lax.dot_general(left, right, (((1,), (1,)), ((), ())), preferred_element_type=F32)


def tokens_product(left, right):
    return lax.dot_general(left, right, (((0,), (0,)), ((), ())), preferred_element_type=F32)


def product(left, right):
    return jnp.dot(left, right, preferred_element_type=F32)


def adamw(weight, first, second, grad, rate):
    first_new = BETA_ONE * first + (1.0 - BETA_ONE) * grad
    second_new = BETA_TWO * second + (1.0 - BETA_TWO) * grad * grad
    ratio = (
        first_new
        / (1.0 - BETA_ONE**STEP)
        / (jnp.sqrt(second_new / (1.0 - BETA_TWO**STEP)) + ADAM_EPSILON)
    )
    return (weight - rate * (ratio + DECAY * weight), first_new, second_new)


def norm_back(grad_in, normed, inverse, gain):
    scaled = grad_in * gain
    return inverse * (scaled - normed * jnp.mean(scaled * normed, axis=-1, keepdims=True))


def exchange(value, axis, bit=1):
    count = lax.axis_size(axis)
    return lax.ppermute(value, axis, [(i, i ^ bit) for i in range(count)])


def shifted(value, step):
    count = lax.axis_size("dp")
    return lax.ppermute(value, "dp", [(i, (i + step) % count) for i in range(count)])


def total_of(terms):
    total = terms[0].astype(F32)
    for term in terms[1:]:
        total = total + term.astype(F32)
    return total


def taken(value, index, axis):
    return lax.dynamic_index_in_dim(value, index, axis, keepdims=True)


def axis_sum(terms, name, axis):
    mine = lax.axis_index(name)
    sent = total_of([taken(term, 1 - mine, axis) for term in terms]).astype(BF16)
    came = exchange(sent, name)
    return [taken(term, mine, axis) for term in terms] + [came]


def dp_sum(value, *ready):
    came = lax.all_to_all(value, "dp", split_axis=0, concat_axis=0, tiled=True)
    if ready:
        came = after(came, *ready)
    return jnp.sum(came.astype(F32), axis=0)


def column_sum(groups, *ready):
    sums = [total_of(terms).astype(BF16) for terms in groups]
    sums = [one.reshape(one.shape[:1] + one.shape[-2:]) for one in sums]
    return dp_sum(jnp.concatenate(sums, axis=2), *ready)


def after(value, *others):
    return lax.optimization_barrier((value,) + others)[0]


def put(whole, piece, *places):
    index = places + (0,) * (whole.ndim - len(places))
    return lax.dynamic_update_slice(whole, piece.reshape((1,) * len(places) + piece.shape), index)


def dp_gather(shard):
    n_dp = lax.axis_size("dp")
    place = lax.axis_index("dp")
    column = put(jnp.zeros((n_dp,) + shard.shape, shard.dtype), shard, place)
    pieces = [shifted(shard, step) for step in range(1, n_dp)]
    for step, piece in enumerate(pieces):
        column = put(column, piece, (place - step - 1) % n_dp)
    return column, pieces


def plane_parts(value):
    middle = value.shape[-1] // 2
    beside = exchange(value, "lo")
    across = exchange(value, "hi")
    corner = [exchange(beside[..., :middle], "hi"), exchange(across[..., middle:], "lo")]
    return [[value], [beside], [across], corner]


def pack_chunks(rows, width, columns):
    full, rest = divmod(width, columns)
    chunks = [(index * rows, rows, 0, 0, index * columns, columns) for index in range(full)]
    if rest:
        count = columns // rest
        part = rows // count
        chunks += [
            (full * rows, part, index * rest, index * part, full * columns, rest)
            for index in range(count)
        ]
    return chunks


def packed_rows(value, columns):
    rows, width = value.shape
    packed = jnp.zeros((rows * width // columns, columns), value.dtype)
    for to_row, count, to_column, row, column, size in pack_chunks(rows, width, columns):
        part = value[row : row + count, column : column + size]
        packed = lax.dynamic_update_slice(packed, part, (to_row, to_column))
    return packed


def unpacked_rows(packed, rows, width):
    columns = packed.shape[-1]
    whole = jnp.zeros(packed.shape[:-2] + (rows, width), packed.dtype)
    lead = (0,) * (packed.ndim - 2)
    for to_row, count, to_column, row, column, size in pack_chunks(rows, width, columns):
        part = packed[..., to_row : to_row + count, to_column : to_column + size]
        whole = lax.dynamic_update_slice(whole, part, lead + (row, column))
    return whole


def relative_gather(value):
    pieces = [value]
    bit = 1
    while bit < lax.axis_size("tp"):
        pieces = pieces + [exchange(piece, "tp", bit) for piece in pieces]
        bit *= 2
    return pieces


def relative_sum(pieces):
    pieces = list(pieces)
    bit = len(pieces) // 2
    while bit:
        for index in range(bit):
            came = exchange(pieces[index + bit].astype(BF16), "tp", bit)
            pieces[index] = pieces[index].astype(F32) + came.astype(F32)
        bit //= 2
    return pieces[0]


def group_gather(value):
    if lax.axis_size("tp") != 2:
        return lax.all_gather(value, "tp", axis=0, tiled=True)
    came = exchange(value, "tp")
    first = lax.axis_index("tp") == 0
    return jnp.concatenate([jnp.where(first, value, came), jnp.where(first, came, value)], axis=0)


def group_swap(value):
    if lax.axis_size("tp") != 2:
        return lax.all_to_all(value, "tp", split_axis=0, concat_axis=0, tiled=True)
    me = lax.axis_index("tp")
    mine = taken(value, me, 0)
    came = exchange(taken(value, 1 - me, 0), "tp")
    return jnp.concatenate([jnp.where(me == 0, mine, came), jnp.where(me == 0, came, mine)], axis=0)


CTX = ("hi", "lo", "tp")


def ctx_swap(value):
    return lax.all_to_all(value, CTX, split_axis=0, concat_axis=0, tiled=True)


def stream_moves(batches):
    group = lax.axis_size("tp")
    count = batches * group
    return [
        [(i, group * ((i + step) % batches) + i // batches) for i in range(count)]
        for step in range(batches)
    ]


def to_streams(value):
    batches = value.shape[0]
    me = lax.axis_index(CTX)
    stream = me // lax.axis_size("tp")
    whole = jnp.zeros_like(value)
    for step, pairs in enumerate(stream_moves(batches)):
        piece = lax.ppermute(taken(value, (me + step) % batches, 0), CTX, pairs)
        whole = lax.dynamic_update_slice_in_dim(whole, piece, (stream - step) % batches, 0)
    return whole


def from_streams(value):
    batches = value.shape[0]
    me = lax.axis_index(CTX)
    stream = me // lax.axis_size("tp")
    whole = jnp.zeros_like(value)
    for step, pairs in enumerate(stream_moves(batches)):
        back = [(b, a) for a, b in pairs]
        piece = lax.ppermute(taken(value, (stream - step) % batches, 0), CTX, back)
        whole = lax.dynamic_update_slice_in_dim(whole, piece, (me + step) % batches, 0)
    return whole


GROUP = HEADS // KV_HEADS
SLOTS = GROUP + 2
JOINED = SLOTS * HEAD_DIM
PAIR = 2


def placement(slots):
    matrix = np.zeros((slots * HEAD_DIM, slots * SLOT), np.float32)
    for slot in range(slots):
        for half in range(2):
            for m in range(HALF):
                matrix[slot * HEAD_DIM + half * HALF + m, slot * SLOT + half * (SLOT // 2) + m] = 1
    return matrix


def mask_of(start, first_row, rows, keys):
    row = first_row + lax.broadcasted_iota(jnp.int32, (rows, keys), 0)
    column = lax.broadcasted_iota(jnp.int32, (rows, keys), 1)
    return (column >= start) & (column <= row)


def columns_of(group, slot):
    first = (group * SLOTS + slot) * SLOT
    return slice(first, first + SLOT)


def forward_kernel(block, joined_ref, table_ref, start_ref, place_ref, back_ref,
                   out_ref, kept_ref, logsum_ref):
    length = joined_ref.shape[0]
    cosine = table_ref[:, :SLOT]
    sine = table_ref[:, SLOT:]
    for group in range(PAIR):
        joined = joined_ref[:, group * JOINED : (group + 1) * JOINED]
        placed = product(joined, place_ref[...])
        for slot in range(SLOTS):
            part = placed[:, slot * SLOT : (slot + 1) * SLOT]
            if slot <= GROUP:
                part = part * cosine + pltpu.roll(part, SLOT // 2, 1) * sine
            if slot < GROUP:
                part = part * (SCALING * LOG2E)
            kept_ref[:, columns_of(group, slot)] = part.astype(BF16)
    lane = lax.broadcasted_iota(jnp.int32, (block, SLOT), 1)
    for first in range(0, length, block):
        rows = slice(first, first + block)
        count = first + block
        mask = mask_of(start_ref[rows, :], first, block, count)
        outs = []
        logsums = jnp.zeros((block, SLOT), F32)
        for group in range(PAIR):
            keys = kept_ref[:count, columns_of(group, GROUP)]
            values = kept_ref[:count, columns_of(group, GROUP + 1)]
            for head in range(GROUP):
                logits = against(kept_ref[rows, columns_of(group, head)], keys)
                logits = jnp.where(mask, logits, -1e30)
                peak = jnp.max(logits, axis=-1, keepdims=True)
                weights = jnp.exp2(logits - peak)
                total = jnp.sum(weights, axis=-1, keepdims=True)
                outs.append((product(weights.astype(BF16), values) / total).astype(BF16))
                logsums = jnp.where(
                    lane == group * GROUP + head, peak + jnp.log2(total), logsums
                )
        logsum_ref[0, rows, :] = logsums
        out_ref[rows, :] = product(jnp.concatenate(outs, axis=1), back_ref[...]).astype(BF16)


def backward_kernel(block, kept_ref, table_ref, start_ref, logsum_ref, att_ref, grad_ref,
                    place_ref, back_ref, out_ref):
    length = kept_ref.shape[0]
    att = product(att_ref[...], place_ref[...])
    grad = product(grad_ref[...], place_ref[...])
    both = att * grad
    grad_low = grad.astype(BF16)
    blocks = length // block

    def add(store, index, value):
        store[index] = value if store[index] is None else store[index] + value

    for group in range(PAIR):
        key_grads = [None] * blocks
        value_grads = [None] * blocks
        query_grads = [[None] * blocks for _ in range(GROUP)]
        for step in range(blocks):
            first = step * block
            rows = slice(first, first + block)
            count = first + block
            mask = mask_of(start_ref[rows, :], first, block, count)
            keys = kept_ref[:count, columns_of(group, GROUP)]
            values = kept_ref[:count, columns_of(group, GROUP + 1)]
            for head in range(GROUP):
                index = group * GROUP + head
                columns = slice(index * SLOT, (index + 1) * SLOT)
                query = kept_ref[rows, columns_of(group, head)]
                delta = jnp.sum(both[rows, columns], axis=-1, keepdims=True)
                logits = against(query, keys)
                weights = jnp.where(
                    mask, jnp.exp2(logits - logsum_ref[0, rows, index : index + 1]), 0.0
                )
                weight_grad = against(grad_low[rows, columns], values)
                logit_grad = (weights * (weight_grad - delta)).astype(BF16)
                query_grads[head][step] = product(logit_grad, keys)
                key_part = tokens_product(logit_grad, query)
                value_part = tokens_product(weights.astype(BF16), grad_low[rows, columns])
                for other in range(step + 1):
                    piece = slice(other * block, (other + 1) * block)
                    add(key_grads, other, key_part[piece])
                    add(value_grads, other, value_part[piece])
        for step in range(blocks):
            rows = slice(step * block, (step + 1) * block)
            cosine = table_ref[rows, :SLOT]
            sine = table_ref[rows, SLOT:]

            def unrotated(value):
                return (value * cosine - pltpu.roll(value, SLOT // 2, 1) * sine).astype(BF16)

            parts = [unrotated(query_grads[head][step] * SCALING) for head in range(GROUP)]
            parts.append(unrotated(key_grads[step] * (1.0 / LOG2E)))
            parts.append(value_grads[step].astype(BF16))
            out_ref[rows, group * JOINED : (group + 1) * JOINED] = product(
                jnp.concatenate(parts, axis=1), back_ref[...]
            ).astype(BF16)


def attention_forward(joined, table, start):
    length, width = joined.shape
    steps = width // (PAIR * JOINED)
    out_width = PAIR * GROUP * HEAD_DIM
    kept_width = PAIR * SLOTS * SLOT
    place = jnp.asarray(placement(SLOTS), BF16)
    back = jnp.asarray(placement(PAIR * GROUP).T, BF16)
    block = min(256, length)
    flops = steps * PAIR * GROUP * length * (length // 2 + block // 2) * SLOT * 4
    return pl.pallas_call(
        functools.partial(forward_kernel, block),
        grid=(steps,),
        in_specs=[
            pl.BlockSpec((length, PAIR * JOINED), lambda s: (0, s)),
            pl.BlockSpec((length, 2 * SLOT), lambda s: (0, 0)),
            pl.BlockSpec((length, 1), lambda s: (0, 0)),
            pl.BlockSpec(place.shape, lambda s: (0, 0)),
            pl.BlockSpec(back.shape, lambda s: (0, 0)),
        ],
        out_specs=[
            pl.BlockSpec((length, out_width), lambda s: (0, s)),
            pl.BlockSpec((length, kept_width), lambda s: (0, s)),
            pl.BlockSpec((1, length, SLOT), lambda s: (s, 0, 0)),
        ],
        out_shape=[
            jax.ShapeDtypeStruct((length, steps * out_width), BF16),
            jax.ShapeDtypeStruct((length, steps * kept_width), BF16),
            jax.ShapeDtypeStruct((steps, length, SLOT), F32),
        ],
        compiler_params=pltpu.CompilerParams(vmem_limit_bytes=VMEM_LIMIT),
        cost_estimate=SMALL_COST,
        name="attention_forward",
    )(joined, table, start, place, back)


def attention_backward(kept, table, start, logsum, att, grad, first, steps):
    length = att.shape[0]
    out_width = PAIR * GROUP * HEAD_DIM
    kept_width = PAIR * SLOTS * SLOT
    place = jnp.asarray(placement(PAIR * GROUP), BF16)
    back = jnp.asarray(placement(SLOTS).T, BF16)
    block = min(256, length)
    flops = steps * PAIR * GROUP * length * (length // 2 + block // 2) * SLOT * 10
    return pl.pallas_call(
        functools.partial(backward_kernel, block),
        grid=(steps,),
        in_specs=[
            pl.BlockSpec((length, kept_width), lambda s: (0, s + first)),
            pl.BlockSpec((length, 2 * SLOT), lambda s: (0, 0)),
            pl.BlockSpec((length, 1), lambda s: (0, 0)),
            pl.BlockSpec((1, length, SLOT), lambda s: (s + first, 0, 0)),
            pl.BlockSpec((length, out_width), lambda s: (0, s + first)),
            pl.BlockSpec((length, out_width), lambda s: (0, s)),
            pl.BlockSpec(place.shape, lambda s: (0, 0)),
            pl.BlockSpec(back.shape, lambda s: (0, 0)),
        ],
        out_specs=pl.BlockSpec((length, PAIR * JOINED), lambda s: (0, s)),
        out_shape=jax.ShapeDtypeStruct((length, steps * PAIR * JOINED), BF16),
        compiler_params=pltpu.CompilerParams(vmem_limit_bytes=VMEM_LIMIT),
        cost_estimate=SMALL_COST,
        name="attention_backward",
    )(kept, table, start, logsum, att, grad, place, back)


def fetched(parts, c_refs, c_ref, sems):
    step = pl.program_id(0)

    def copies(index):
        first = sum(parts[:index])
        column = 0
        for part, ref in enumerate(c_refs[first : first + parts[index]]):
            size = ref.shape[1]
            target = c_ref.at[index % 2, :, pl.ds(column, size)]
            yield pltpu.make_async_copy(ref, target, sems.at[index % 2, part])
            column += size

    for index in range(len(parts)):

        @pl.when(step == index)
        def _():
            if index == 0:
                for copy in copies(0):
                    copy.start()
            if index + 1 < len(parts):
                for copy in copies(index + 1):
                    copy.start()
            for copy in copies(index):
                copy.wait()

    return c_ref[step % 2]


def feed_kernel(parts, residual, fresh, places_ref, *refs):
    c_refs, refs = refs[: sum(parts)], refs[sum(parts) :]
    (dy_ref, expand_ref, down_ref), refs = refs[:3], refs[3:]
    if residual:
        hidden_ref, refs = refs[0], refs[1:]
    if not fresh:
        refs = refs[2:]
    out_ref, terms_ref, dc_ref, c_buffer, sems = refs
    hidden = down_ref.shape[0]
    c = fetched(parts, c_refs, c_buffer, sems)
    gate = product(c, expand_ref[:, :hidden])
    up = product(c, expand_ref[:, hidden:])
    dm = against(dy_ref[0], down_ref[...])
    sigmoid = jax.nn.sigmoid(gate)
    active = gate * sigmoid
    mixed = (active * up).astype(BF16)
    dgate = (dm * up * sigmoid * (1.0 + gate * (1.0 - sigmoid))).astype(BF16)
    dup = (dm * active).astype(BF16)
    terms_ref[0, 0] = mixed
    terms_ref[0, 1] = dgate
    terms_ref[0, 2] = dup
    dc = against(dgate, expand_ref[:, :hidden]) + against(dup, expand_ref[:, hidden:])
    dc_ref[0] = dc.astype(BF16)
    out = product(mixed, down_ref[...])
    if residual:
        out_ref[0] = (out + jnp.where(pl.program_id(0) == 0, hidden_ref[...], 0.0)).astype(BF16)
    else:
        out_ref[0] = out.astype(BF16)


def c_scratch(own, width):
    return [pltpu.VMEM((2, own, width), BF16), pltpu.SemaphoreType.DMA((2, 2))]


def feed_forward(places, c, dy, expand, down, blocks, before=None, hidden_res=None):
    parts = tuple(len(block) for block in c)
    steps = len(c)
    own, width = dy.shape[1] // (blocks // 4), dy.shape[2]
    hidden = down.shape[0]
    residual = hidden_res is not None
    fresh = before is None
    single = pl.Buffered(1)
    whole = lambda s, p: (0, 0)
    token = pl.BlockSpec((1, own, width), lambda s, p: (p[s, 1], p[s, 2], 0))
    flat = [part for block in c for part in block]
    operands = [places, *flat, dy, expand, down]
    in_specs = [pl.BlockSpec(memory_space=pl.ANY)] * len(flat) + [
        token,
        pl.BlockSpec(expand.shape, whole, pipeline_mode=single),
        pl.BlockSpec(down.shape, whole, pipeline_mode=single),
    ]
    if residual:
        operands.append(hidden_res)
        in_specs.append(pl.BlockSpec((own, width), whole, pipeline_mode=single))
    aliases = {}
    if not fresh:
        aliases = {len(operands): 0, len(operands) + 1: 1}
        operands += list(before)
        in_specs += [pl.BlockSpec(memory_space=pl.ANY)] * 2
    return pl.pallas_call(
        functools.partial(feed_kernel, parts, residual, fresh),
        grid_spec=pltpu.PrefetchScalarGridSpec(
            num_scalar_prefetch=1,
            grid=(steps,),
            in_specs=in_specs,
            out_specs=[
                token,
                pl.BlockSpec((1, 3, own, hidden), lambda s, p: (p[s, 0], 0, 0, 0)),
                pl.BlockSpec((1, own, width), lambda s, p: (s, 0, 0)),
            ],
            scratch_shapes=c_scratch(own, width),
        ),
        out_shape=[
            jax.ShapeDtypeStruct(dy.shape, BF16),
            jax.ShapeDtypeStruct((blocks, 3, own, hidden), BF16),
            jax.ShapeDtypeStruct((steps, own, width), BF16),
        ],
        input_output_aliases=aliases,
        compiler_params=pltpu.CompilerParams(vmem_limit_bytes=VMEM_LIMIT),
        cost_estimate=SMALL_COST,
        name="feed_forward",
    )(*operands)


def accumulate(total_ref, value, columns=slice(None)):
    @pl.when(pl.program_id(0) == 0)
    def _():
        total_ref[:, columns] = value

    @pl.when(pl.program_id(0) > 0)
    def _():
        total_ref[:, columns] += value


def down_grad_kernel(rows, places_ref, dy_ref, mixed_ref, out_ref, total_ref):
    accumulate(total_ref, tokens_product(mixed_ref[0, 0], dy_ref[0]))
    width, columns = total_ref.shape[1], out_ref.shape[2]

    @pl.when(pl.program_id(0) == pl.num_programs(0) - 1)
    def _():
        for place in range(out_ref.shape[0]):
            for to_row, count, to_column, row, column, size in pack_chunks(rows, width, columns):
                first = place * rows + row
                out_ref[place, to_row : to_row + count, to_column : to_column + size] = total_ref[
                    first : first + count, column : column + size
                ].astype(BF16)


def expand_grad_kernel(parts, places_ref, *refs):
    c_refs, refs = refs[: sum(parts)], refs[sum(parts) :]
    dgate_ref, dup_ref, _, out_ref, total_ref, c_buffer, sems = refs
    hidden = dgate_ref.shape[3]
    c = fetched(parts, c_refs, c_buffer, sems)
    accumulate(total_ref, tokens_product(c, dgate_ref[0, 0]), slice(0, hidden))
    accumulate(total_ref, tokens_product(c, dup_ref[0, 0]), slice(hidden, None))

    @pl.when(pl.program_id(0) == pl.num_programs(0) - 1)
    def _():
        out_ref[...] = total_ref[...].astype(BF16).reshape(out_ref.shape)


def down_grads(places, dy, terms, n_dp, rows_before):
    blocks, _, own, hidden = terms.shape
    width = dy.shape[2]
    packed = hidden * width // (2 * hidden) // n_dp
    return pl.pallas_call(
        functools.partial(down_grad_kernel, hidden // n_dp),
        grid_spec=pltpu.PrefetchScalarGridSpec(
            num_scalar_prefetch=1,
            grid=(blocks,),
            in_specs=[
                pl.BlockSpec((1, own, width), lambda s, p: (p[s, 1], p[s, 2], 0)),
                pl.BlockSpec((1, 1, own, hidden), lambda s, p: (p[s, 0], 0, 0, 0)),
            ],
            out_specs=pl.BlockSpec(
                (n_dp, packed, 2 * hidden),
                lambda s, p: (0, rows_before // packed, 0),
                pipeline_mode=pl.Buffered(1),
            ),
            scratch_shapes=[pltpu.VMEM((hidden, width), F32)],
        ),
        out_shape=jax.ShapeDtypeStruct((n_dp, rows_before + packed, 2 * hidden), BF16),
        compiler_params=pltpu.CompilerParams(vmem_limit_bytes=VMEM_LIMIT),
        cost_estimate=SMALL_COST,
        name="down_grads",
    )(places, dy, terms)


def expand_grads(places, c, terms, packed, rows):
    parts = tuple(len(block) for block in c)
    blocks, _, own, hidden = terms.shape
    n_dp = packed.shape[0]
    width = n_dp * rows
    flat = [part for block in c for part in block]
    return pl.pallas_call(
        functools.partial(expand_grad_kernel, parts),
        grid_spec=pltpu.PrefetchScalarGridSpec(
            num_scalar_prefetch=1,
            grid=(blocks,),
            in_specs=[pl.BlockSpec(memory_space=pl.ANY)] * len(flat)
            + [
                pl.BlockSpec((1, 1, own, hidden), lambda s, p: (p[s, 0], 1, 0, 0)),
                pl.BlockSpec((1, 1, own, hidden), lambda s, p: (p[s, 0], 2, 0, 0)),
                pl.BlockSpec(memory_space=pl.ANY),
            ],
            out_specs=pl.BlockSpec(
                (n_dp, rows, 2 * hidden), lambda s, p: (0, 0, 0), pipeline_mode=pl.Buffered(1)
            ),
            scratch_shapes=[pltpu.VMEM((width, 2 * hidden), F32)] + c_scratch(own, width),
        ),
        out_shape=jax.ShapeDtypeStruct(packed.shape, BF16),
        input_output_aliases={1 + len(flat) + 2: 0},
        compiler_params=pltpu.CompilerParams(vmem_limit_bytes=VMEM_LIMIT),
        cost_estimate=SMALL_COST,
        name="expand_grads",
    )(places, *flat, terms, terms, packed)


def local(
    inputs,
    doc_ids,
    cotangent,
    attend_in,
    attend_out,
    gains,
    expand,
    contract,
    attend_in_first,
    attend_in_second,
    attend_out_first,
    attend_out_second,
    gains_first,
    gains_second,
    expand_first,
    expand_second,
    contract_first,
    contract_second,
):
    batches, rows_local, width = inputs.shape
    n_tp = lax.axis_size("tp")
    n_dp = lax.axis_size("dp")
    me = lax.axis_index("tp")
    stream_place = lax.axis_index(("hi", "lo")).astype(jnp.int32)
    stream = rows_local * batches * n_tp
    own = stream // n_tp
    qwidth = HEADS * HEAD_DIM
    kwidth = KV_HEADS * HEAD_DIM
    joined_width = qwidth + 2 * kwidth
    part_in = joined_width // n_tp
    part_out = width // n_tp
    row_in = attend_in.shape[0]
    row_down = contract.shape[0]

    def to_groups(value):
        rows = value.shape[0]
        return jnp.concatenate(
            [
                value[:, :qwidth].reshape(rows, KV_HEADS, -1),
                value[:, qwidth : qwidth + kwidth].reshape(rows, KV_HEADS, -1),
                value[:, qwidth + kwidth :].reshape(rows, KV_HEADS, -1),
            ],
            axis=2,
        ).reshape(rows, joined_width)

    def from_groups(value):
        rows = value.shape[0]
        grid = value.reshape(rows, KV_HEADS, JOINED)
        first, second = GROUP * HEAD_DIM, (GROUP + 1) * HEAD_DIM
        return jnp.concatenate(
            [
                grid[:, :, :first].reshape(rows, qwidth),
                grid[:, :, first:second].reshape(rows, kwidth),
                grid[:, :, second:].reshape(rows, kwidth),
            ],
            axis=1,
        )

    gain_columns = jnp.concatenate([gains.T, jnp.zeros((row_in, SLOT - 2), F32)], axis=1)
    attend_shard = jnp.concatenate([to_groups(attend_in), gain_columns, attend_out], axis=1)
    attend_all = lax.all_gather(
        attend_shard.astype(BF16), ("dp", "hi", "lo", "tp"), axis=0, tiled=True
    )

    n_ctx = 4 * n_tp
    expand_parts = expand.astype(BF16).reshape(row_in, 2, n_dp, n_ctx, row_down)
    expand_parts = expand_parts.transpose(3, 0, 1, 2, 4).reshape(n_ctx, row_in, -1)
    expand_shard = ctx_swap(expand_parts).reshape(n_ctx * row_in, -1)
    hidden_two = expand_shard.shape[1]
    rows_expand = n_ctx * row_in
    feed_shard = jnp.concatenate(
        [expand_shard, packed_rows(contract.astype(BF16), hidden_two)], axis=0
    )
    feed_all, feed_pieces = dp_gather(after(feed_shard, attend_all))
    expand_all = feed_all[:, :rows_expand].reshape(width, hidden_two)
    down_all = unpacked_rows(feed_all[:, rows_expand:], row_down, width).reshape(-1, width)

    ids_wide = jnp.broadcast_to(doc_ids[:, :, None].astype(BF16), (batches, rows_local, SLOT))
    moved = to_streams(jnp.concatenate([inputs, ids_wide], axis=2)).reshape(own, width + SLOT)
    resid = moved[:, :width]
    moved_all = group_gather(moved)
    resid_all = moved_all[:, :width].astype(F32)
    ids = moved_all[:, width].astype(jnp.int32)
    dy_all = lax.all_gather(after(cotangent, moved), CTX, axis=1, tiled=True)

    start = jnp.sum((ids[None, :] < ids[:, None]).astype(jnp.int32), axis=-1)
    position = (jnp.arange(stream, dtype=jnp.int32) - start).astype(F32)
    inverse = jnp.power(ROPE_BASE, -2.0 * jnp.arange(HALF, dtype=F32) / HEAD_DIM)
    angles = position[:, None] * inverse
    cosine = jnp.cos(angles)
    sine = jnp.sin(angles)
    gap = jnp.zeros((stream, SLOT // 2 - HALF), F32)
    table = jnp.concatenate([cosine, gap, cosine, gap, -sine, gap, sine, gap], axis=-1)
    start = start[:, None]

    in_low = lax.dynamic_slice(attend_all, (0, me * part_in), (width, part_in))
    gain_one = attend_all[:, joined_width].astype(F32)
    gain_two = attend_all[:, joined_width + 1].astype(F32)
    out_low = lax.dynamic_slice(
        attend_all, (me * (qwidth // n_tp), joined_width + SLOT), (qwidth // n_tp, width)
    )

    inv_all = lax.rsqrt(jnp.mean(resid_all * resid_all, axis=-1, keepdims=True) + EPSILON)
    first_in = (resid_all * inv_all * gain_one).astype(BF16)
    joined = product(first_in, in_low).astype(BF16)
    att_low, kept, logsum = attention_forward(joined, table, start)
    att_low = after(att_low, feed_pieces[0])

    def own_sum(value):
        grid = value.reshape(n_tp, own, width)
        if n_tp != 2:
            return lax.psum_scatter(grid, "tp", scatter_dimension=0, tiled=True)[0].astype(F32)
        came = exchange(lax.dynamic_index_in_dim(grid, 1 - me, 0, keepdims=False), "tp")
        mine = lax.dynamic_index_in_dim(grid, me, 0, keepdims=False)
        return mine.astype(F32) + came.astype(F32)

    resid = resid.astype(F32)
    hidden_res = resid + own_sum(product(att_low, out_low).astype(BF16))
    inv_two = lax.rsqrt(jnp.mean(hidden_res * hidden_res, axis=-1, keepdims=True) + EPSILON)
    normed_two = hidden_res * inv_two
    second_in = (normed_two * gain_two).astype(BF16)
    def place_row(relative, member):
        return jnp.stack(
            [jnp.int32(relative * n_tp + member), stream_place ^ relative, me ^ member]
        ).astype(jnp.int32)

    blocks = 4 * n_tp
    parts = [
        [relative_gather(part) for part in chip] for chip in plane_parts(second_in)
    ]

    def pieces_of(relative, member):
        return [part[member] for part in parts[relative]]

    def feed_call(order, before=None, residual=None):
        rows = jnp.stack([place_row(relative, member) for relative, member in order])
        c = [pieces_of(relative, member) for relative, member in order]
        return feed_forward(rows, c, dy_all, expand_all, down_all, blocks, before, residual)

    near_order = [(0, member) for member in range(n_tp)]
    first_order = [(r, member) for member in range(1, n_tp) for r in (1, 2, 3)]
    second_order = [(r, 0) for r in (1, 2, 3)]
    out_all, terms, first_dc = feed_call(first_order)
    first_dc = first_dc.reshape(n_tp - 1, 3, own, width)
    first_sent = [first_dc[member] for member in range(n_tp - 1)]
    out_all, terms, second_dc = feed_call(second_order, (out_all, terms))
    far_sum = relative_sum([second_dc] + first_sent).astype(BF16)
    middle = width // 2
    left_sent, right_sent = far_sum[0::2, :, :middle], far_sum[1:, :, middle:]
    out_all, terms, near_dc = feed_call(
        near_order, lax.optimization_barrier((out_all, terms, left_sent, right_sent))[:2], hidden_res
    )
    every_order = near_order + first_order + second_order
    every_rows = jnp.stack([place_row(relative, member) for relative, member in every_order])
    packed = down_grads(every_rows, dy_all, terms, n_dp, rows_expand)
    near = relative_sum([near_dc[member] for member in range(n_tp)])
    left_came = after(exchange(left_sent, "lo"), packed)
    right_came = after(exchange(right_sent, "hi"), packed)
    left = total_of([far_sum[1, :, :middle], left_came[1]]).astype(BF16)
    right = total_of([far_sum[0, :, middle:], right_came[1]]).astype(BF16)
    feed_terms = expand_grads(
        every_rows,
        [pieces_of(relative, member) for relative, member in every_order],
        terms,
        after(packed, left, right),
        rows_expand,
    )
    left = after(exchange(left, "hi"), feed_terms)
    right = after(exchange(right, "lo"), feed_terms)
    second_grad = near.astype(F32) + jnp.concatenate(
        [total_of([left_came[0], left]), total_of([right_came[0], right])], axis=1
    )
    out_all, second_grad = lax.optimization_barrier((out_all, second_grad))
    block_out = lax.psum_scatter(out_all, CTX, scatter_dimension=1, tiled=True)

    upstream = lax.dynamic_slice(dy_all, (stream_place, me * own, 0), (1, own, width))[0]
    upstream = upstream.astype(F32)
    hidden_grad = upstream + norm_back(second_grad, normed_two, inv_two, gain_two)
    branch_all = group_gather(hidden_grad.astype(BF16))
    att_steps = logsum.shape[0]
    cuts = [0, att_steps // 2, att_steps] if att_steps > 1 else [0, 1]
    heads_width = PAIR * GROUP * HEAD_DIM
    def plane_stage(terms, name):
        return axis_sum(terms, name, 1 if name == "hi" else 2)

    def plane_grid(value):
        return [value.reshape(n_dp, 2, 2, n_tp * row_in, -1)]

    def plane_terms(value, order):
        return plane_stage(plane_stage(plane_grid(value), order[0]), order[1])

    orders = (("hi", "lo"), ("lo", "hi"))

    def heads_grad(index):
        part = out_low[cuts[index] * heads_width : cuts[index + 1] * heads_width]
        return against(branch_all, part).astype(BF16)

    def heads_back(index, grad):
        begin, end = cuts[index], cuts[index + 1]
        return attention_backward(kept, table, start, logsum, att_low, grad, begin, end - begin)

    dp_place = lax.axis_index("dp")

    def feed_piece(step):
        return lax.dynamic_index_in_dim(feed_terms, (dp_place + step) % n_dp, 0, keepdims=False)

    feed_came = [shifted(feed_piece(step), step) for step in range(1, n_dp)]

    joined_parts = [heads_back(0, heads_grad(0))]
    in_parts = [tokens_product(first_in, joined_parts[0]).astype(BF16)]

    branch_late = after(branch_all, joined_parts[0])
    if n_tp == 2:
        heads_rows = qwidth // n_tp

        def out_columns(member):
            part = lax.dynamic_slice_in_dim(branch_late, member * part_out, part_out, 1)
            return tokens_product(att_low, part).astype(BF16)

        out_came = exchange(out_columns(1 - me), "tp")
        out_term = jnp.zeros((qwidth, part_out), BF16)
        out_term = lax.dynamic_update_slice_in_dim(out_term, out_columns(me), me * heads_rows, 0)
        out_term = lax.dynamic_update_slice_in_dim(out_term, out_came, (1 - me) * heads_rows, 0)
    else:
        out_term = tokens_product(att_low, branch_late).astype(BF16)
        out_term = out_term.reshape(qwidth // n_tp, n_tp, part_out).transpose(1, 0, 2)
        out_term = group_swap(out_term).reshape(qwidth, part_out)
    half = part_out // 2
    out_parts = [out_term[:, :half], out_term[:, half:]]

    if len(cuts) > 2:
        grad = after(heads_grad(1), in_parts[0], out_term)
        joined_parts.append(heads_back(1, grad))
    in_terms = [plane_stage(plane_grid(in_parts[0]), orders[0][0])]
    in_terms[0][-1] = after(in_terms[0][-1], feed_came[0])
    if len(cuts) > 2:
        in_parts.append(tokens_product(first_in, joined_parts[1]).astype(BF16))
        in_terms.append(plane_stage(plane_grid(in_parts[1]), orders[1][0]))
        in_terms[-1][-1] = after(in_terms[-1][-1], feed_came[1])
    out_terms = [
        plane_stage(plane_grid(after(part, in_parts[-1])), order[0])
        for part, order in zip(out_parts, orders)
    ]
    in_terms = [plane_stage(terms, order[1]) for terms, order in zip(in_terms, orders)]
    out_terms = [plane_stage(terms, order[1]) for terms, order in zip(out_terms, orders)]
    joined_all = after(jnp.concatenate(joined_parts, axis=1), in_parts[-1])
    first_part = against(joined_all, in_low).astype(BF16)

    ready = (first_part,) + tuple(terms[-1] for terms in in_terms)
    low = F32 if n_tp != 2 else BF16

    def owned(terms):
        rows = column_sum(terms).reshape(n_tp, row_in, -1)
        return group_swap(rows.astype(low)).astype(F32).transpose(1, 0, 2).reshape(row_in, -1)

    in_sum = owned(in_terms)
    out_terms[-1][-1] = after(out_terms[-1][-1], in_sum)
    out_sum = owned(out_terms)
    feed_sum = total_of([feed_piece(0)] + [after(came, in_sum) for came in feed_came])
    expand_rows = feed_sum[:rows_expand].astype(BF16).reshape(n_ctx, row_in, -1)
    expand_sum = ctx_swap(after(expand_rows, in_sum)).reshape(n_ctx, row_in, 2, n_dp, row_down)
    expand_sum = expand_sum.transpose(1, 2, 3, 0, 4).reshape(row_in, 2 * FF).astype(F32)
    contract_sum = unpacked_rows(feed_sum[rows_expand:], row_down, width)

    inv_one = lax.rsqrt(jnp.mean(resid * resid, axis=-1, keepdims=True) + EPSILON)
    first_grad = own_sum(first_part)
    first_grad = after(first_grad, *ready[1:])
    resid_grad = hidden_grad + norm_back(first_grad, resid * inv_one, inv_one, gain_one)
    shape = (batches, rows_local, width)
    grad_inputs = from_streams(resid_grad.astype(BF16).reshape(shape))

    in_sum = from_groups(in_sum)
    low_gains = gains.astype(BF16).astype(F32)
    gain_sum = jnp.stack(
        [
            jnp.sum(in_sum * attend_in.astype(BF16).astype(F32), axis=1),
            jnp.sum(expand_sum * expand.astype(BF16).astype(F32), axis=1),
        ]
    ) / low_gains

    out_fan = max(1, HEADS * HEAD_DIM // (stream // 8))
    new_in = adamw(attend_in, attend_in_first, attend_in_second, in_sum, RATE / math.sqrt(D))
    new_out = adamw(
        attend_out, attend_out_first, attend_out_second, out_sum, RATE / math.sqrt(out_fan)
    )
    new_gain = adamw(gains, gains_first, gains_second, gain_sum, GAIN_RATE)
    new_expand = adamw(expand, expand_first, expand_second, expand_sum, RATE / math.sqrt(D))
    new_contract = adamw(
        contract, contract_first, contract_second, contract_sum, RATE / math.sqrt(FF)
    )
    return (block_out, grad_inputs, *new_in, *new_out, *new_gain, *new_expand, *new_contract)


def solution(mesh):
    n_dp, n_ctx = mesh.shape["dp"], mesh.shape["ctx"]
    cut = jax.sharding.Mesh(
        mesh.devices.reshape(n_dp, 2, 2, n_ctx // 4), ("dp", "hi", "lo", "tp")
    )
    every = ("dp", "hi", "lo", "tp")
    rows = P(every, None)
    columns = P(None, every)
    tokens = P(None, every, None)
    return jax.shard_map(
        local,
        mesh=cut,
        in_specs=(tokens, columns, tokens, rows, rows, columns, rows, rows)
        + (rows,) * 4
        + (columns,) * 2
        + (rows,) * 4,
        out_specs=(tokens, tokens) + (rows,) * 6 + (columns,) * 3 + (rows,) * 6,
        check_vma=False,
    )
```

```python
import functools
import math

import jax
import jax.numpy as jnp
import numpy as np
from jax import lax
from jax.experimental import pallas as pl
from jax.experimental.pallas import tpu as pltpu
from jax.sharding import PartitionSpec as P

D = 1536
HEADS = 16
KV_HEADS = 8
HEAD_DIM = 96
FF = 4096
STEP = 10

EPSILON = 1e-06
ROPE_BASE = 100000.0
BETA_ONE = 0.9
BETA_TWO = 0.95
ADAM_EPSILON = 1e-08
DECAY = 0.1
RATE = 0.3
GAIN_RATE = 0.25

HALF = HEAD_DIM // 2
SLOT = 128
SCALING = HEAD_DIM ** (-0.5)
LOG2E = math.log2(math.e)
VMEM_LIMIT = 60 * 1024 * 1024
BF16 = jnp.bfloat16
F32 = jnp.float32
SMALL_COST = pl.CostEstimate(flops=1 << 20, bytes_accessed=1 << 20, transcendentals=0)


def against(left, right):
    return lax.dot_general(left, right, (((1,), (1,)), ((), ())), preferred_element_type=F32)


def tokens_product(left, right):
    return lax.dot_general(left, right, (((0,), (0,)), ((), ())), preferred_element_type=F32)


def product(left, right):
    return jnp.dot(left, right, preferred_element_type=F32)


def adamw(weight, first, second, grad, rate):
    first_new = BETA_ONE * first + (1.0 - BETA_ONE) * grad
    second_new = BETA_TWO * second + (1.0 - BETA_TWO) * grad * grad
    ratio = (
        first_new
        / (1.0 - BETA_ONE**STEP)
        / (jnp.sqrt(second_new / (1.0 - BETA_TWO**STEP)) + ADAM_EPSILON)
    )
    return (weight - rate * (ratio + DECAY * weight), first_new, second_new)


def norm_back(grad_in, normed, inverse, gain):
    scaled = grad_in * gain
    return inverse * (scaled - normed * jnp.mean(scaled * normed, axis=-1, keepdims=True))


def exchange(value, axis, bit=1):
    count = lax.axis_size(axis)
    return lax.ppermute(value, axis, [(i, i ^ bit) for i in range(count)])


def shifted(value, step):
    count = lax.axis_size("dp")
    return lax.ppermute(value, "dp", [(i, (i + step) % count) for i in range(count)])


def total_of(terms):
    total = terms[0].astype(F32)
    for term in terms[1:]:
        total = total + term.astype(F32)
    return total


def taken(value, index, axis):
    return lax.dynamic_index_in_dim(value, index, axis, keepdims=True)


def axis_sum(terms, name, axis):
    mine = lax.axis_index(name)
    sent = total_of([taken(term, 1 - mine, axis) for term in terms]).astype(BF16)
    came = exchange(sent, name)
    return [taken(term, mine, axis) for term in terms] + [came]


def dp_sum(value, *ready):
    came = lax.all_to_all(value, "dp", split_axis=0, concat_axis=0, tiled=True)
    if ready:
        came = after(came, *ready)
    return jnp.sum(came.astype(F32), axis=0)


def column_sum(groups, *ready):
    sums = [total_of(terms).astype(BF16) for terms in groups]
    sums = [one.reshape(one.shape[:1] + one.shape[-2:]) for one in sums]
    return dp_sum(jnp.concatenate(sums, axis=2), *ready)


def after(value, *others):
    return lax.optimization_barrier((value,) + others)[0]


def put(whole, piece, *places):
    index = places + (0,) * (whole.ndim - len(places))
    return lax.dynamic_update_slice(whole, piece.reshape((1,) * len(places) + piece.shape), index)


def dp_gather(shard):
    n_dp = lax.axis_size("dp")
    place = lax.axis_index("dp")
    column = put(jnp.zeros((n_dp,) + shard.shape, shard.dtype), shard, place)
    pieces = [shifted(shard, step) for step in range(1, n_dp)]
    for step, piece in enumerate(pieces):
        column = put(column, piece, (place - step - 1) % n_dp)
    return column, pieces


def plane_parts(value):
    middle = value.shape[-1] // 2
    beside = exchange(value, "lo")
    across = exchange(value, "hi")
    corner = [exchange(beside[..., :middle], "hi"), exchange(across[..., middle:], "lo")]
    return [[value], [beside], [across], corner]


def pack_chunks(rows, width, columns):
    full, rest = divmod(width, columns)
    chunks = [(index * rows, rows, 0, 0, index * columns, columns) for index in range(full)]
    if rest:
        count = columns // rest
        part = rows // count
        chunks += [
            (full * rows, part, index * rest, index * part, full * columns, rest)
            for index in range(count)
        ]
    return chunks


def packed_rows(value, columns):
    rows, width = value.shape
    packed = jnp.zeros((rows * width // columns, columns), value.dtype)
    for to_row, count, to_column, row, column, size in pack_chunks(rows, width, columns):
        part = value[row : row + count, column : column + size]
        packed = lax.dynamic_update_slice(packed, part, (to_row, to_column))
    return packed


def unpacked_rows(packed, rows, width):
    columns = packed.shape[-1]
    whole = jnp.zeros(packed.shape[:-2] + (rows, width), packed.dtype)
    lead = (0,) * (packed.ndim - 2)
    for to_row, count, to_column, row, column, size in pack_chunks(rows, width, columns):
        part = packed[..., to_row : to_row + count, to_column : to_column + size]
        whole = lax.dynamic_update_slice(whole, part, lead + (row, column))
    return whole


def relative_gather(value):
    pieces = [value]
    bit = 1
    while bit < lax.axis_size("tp"):
        pieces = pieces + [exchange(piece, "tp", bit) for piece in pieces]
        bit *= 2
    return pieces


def relative_sum(pieces, arrived=False):
    pieces = list(pieces)
    if arrived:
        return total_of(pieces)
    bit = len(pieces) // 2
    while bit:
        for index in range(bit):
            came = exchange(pieces[index + bit].astype(BF16), "tp", bit)
            pieces[index] = pieces[index].astype(F32) + came.astype(F32)
        bit //= 2
    return pieces[0]


def group_gather(value):
    if lax.axis_size("tp") != 2:
        return lax.all_gather(value, "tp", axis=0, tiled=True)
    came = exchange(value, "tp")
    first = lax.axis_index("tp") == 0
    return jnp.concatenate([jnp.where(first, value, came), jnp.where(first, came, value)], axis=0)


def group_swap(value):
    if lax.axis_size("tp") != 2:
        return lax.all_to_all(value, "tp", split_axis=0, concat_axis=0, tiled=True)
    me = lax.axis_index("tp")
    mine = taken(value, me, 0)
    came = exchange(taken(value, 1 - me, 0), "tp")
    return jnp.concatenate([jnp.where(me == 0, mine, came), jnp.where(me == 0, came, mine)], axis=0)


CTX = ("hi", "lo", "tp")


def ctx_swap(value):
    return lax.all_to_all(value, CTX, split_axis=0, concat_axis=0, tiled=True)


def stream_moves(batches):
    group = lax.axis_size("tp")
    count = batches * group
    return [
        [(i, group * ((i + step) % batches) + i // batches) for i in range(count)]
        for step in range(batches)
    ]


def to_streams(value):
    batches = value.shape[0]
    me = lax.axis_index(CTX)
    stream = me // lax.axis_size("tp")
    whole = jnp.zeros_like(value)
    for step, pairs in enumerate(stream_moves(batches)):
        piece = lax.ppermute(taken(value, (me + step) % batches, 0), CTX, pairs)
        whole = lax.dynamic_update_slice_in_dim(whole, piece, (stream - step) % batches, 0)
    return whole


def from_streams(value):
    batches = value.shape[0]
    me = lax.axis_index(CTX)
    stream = me // lax.axis_size("tp")
    whole = jnp.zeros_like(value)
    for step, pairs in enumerate(stream_moves(batches)):
        back = [(b, a) for a, b in pairs]
        piece = lax.ppermute(taken(value, (stream - step) % batches, 0), CTX, back)
        whole = lax.dynamic_update_slice_in_dim(whole, piece, (me + step) % batches, 0)
    return whole


GROUP = HEADS // KV_HEADS
SLOTS = GROUP + 2
JOINED = SLOTS * HEAD_DIM
PAIR = 2


def placement(slots):
    matrix = np.zeros((slots * HEAD_DIM, slots * SLOT), np.float32)
    for slot in range(slots):
        for half in range(2):
            for m in range(HALF):
                matrix[slot * HEAD_DIM + half * HALF + m, slot * SLOT + half * (SLOT // 2) + m] = 1
    return matrix


def mask_of(start, first_row, rows, keys):
    row = first_row + lax.broadcasted_iota(jnp.int32, (rows, keys), 0)
    column = lax.broadcasted_iota(jnp.int32, (rows, keys), 1)
    return (column >= start) & (column <= row)


def columns_of(group, slot):
    first = (group * SLOTS + slot) * SLOT
    return slice(first, first + SLOT)


def forward_kernel(block, member_ref, input_ref, weight_ref, table_ref, start_ref, place_ref,
                   back_ref, head_ref, out_ref, kept_ref, logsum_ref, part_ref, total_ref):
    length = input_ref.shape[0]
    cosine = table_ref[:, :SLOT]
    sine = table_ref[:, SLOT:]
    for group in range(PAIR):
        weight = weight_ref[:, group * JOINED : (group + 1) * JOINED]
        joined = product(input_ref[...], weight).astype(BF16)
        placed = product(joined, place_ref[...])
        for slot in range(SLOTS):
            part = placed[:, slot * SLOT : (slot + 1) * SLOT]
            if slot <= GROUP:
                part = part * cosine + pltpu.roll(part, SLOT // 2, 1) * sine
            if slot < GROUP:
                part = part * (SCALING * LOG2E)
            kept_ref[:, columns_of(group, slot)] = part.astype(BF16)
    lane = lax.broadcasted_iota(jnp.int32, (block, SLOT), 1)
    for first in range(0, length, block):
        rows = slice(first, first + block)
        count = first + block
        mask = mask_of(start_ref[rows, :], first, block, count)
        outs = []
        logsums = jnp.zeros((block, SLOT), F32)
        for group in range(PAIR):
            keys = kept_ref[:count, columns_of(group, GROUP)]
            values = kept_ref[:count, columns_of(group, GROUP + 1)]
            for head in range(GROUP):
                logits = against(kept_ref[rows, columns_of(group, head)], keys)
                logits = jnp.where(mask, logits, -1e30)
                peak = jnp.max(logits, axis=-1, keepdims=True)
                weights = jnp.exp2(logits - peak)
                total = jnp.sum(weights, axis=-1, keepdims=True)
                outs.append((product(weights.astype(BF16), values) / total).astype(BF16))
                logsums = jnp.where(
                    lane == group * GROUP + head, peak + jnp.log2(total), logsums
                )
        logsum_ref[0, rows, :] = logsums
        compact = product(jnp.concatenate(outs, axis=1), back_ref[...]).astype(BF16)
        out_ref[rows, :] = compact
        part = product(compact, head_ref[...])

        @pl.when(pl.program_id(0) == 0)
        def _():
            total_ref[rows, :] = part

        @pl.when(pl.program_id(0) > 0)
        def _():
            total_ref[rows, :] += part

    @pl.when(pl.program_id(0) == pl.num_programs(0) - 1)
    def _():
        part_ref[...] = total_ref[...].astype(BF16)


def backward_kernel(block, kept_ref, table_ref, start_ref, logsum_ref, att_ref, branch_ref,
                    head_ref, place_ref, back_ref, out_ref):
    length = kept_ref.shape[0]
    att = product(att_ref[...], place_ref[...])
    grad = product(against(branch_ref[...], head_ref[...]).astype(BF16), place_ref[...])
    both = att * grad
    grad_low = grad.astype(BF16)
    blocks = length // block

    def add(store, index, value):
        store[index] = value if store[index] is None else store[index] + value

    for group in range(PAIR):
        key_grads = [None] * blocks
        value_grads = [None] * blocks
        query_grads = [[None] * blocks for _ in range(GROUP)]
        for step in range(blocks):
            first = step * block
            rows = slice(first, first + block)
            count = first + block
            mask = mask_of(start_ref[rows, :], first, block, count)
            keys = kept_ref[:count, columns_of(group, GROUP)]
            values = kept_ref[:count, columns_of(group, GROUP + 1)]
            for head in range(GROUP):
                index = group * GROUP + head
                columns = slice(index * SLOT, (index + 1) * SLOT)
                query = kept_ref[rows, columns_of(group, head)]
                delta = jnp.sum(both[rows, columns], axis=-1, keepdims=True)
                logits = against(query, keys)
                weights = jnp.where(
                    mask, jnp.exp2(logits - logsum_ref[0, rows, index : index + 1]), 0.0
                )
                weight_grad = against(grad_low[rows, columns], values)
                logit_grad = (weights * (weight_grad - delta)).astype(BF16)
                query_grads[head][step] = product(logit_grad, keys)
                key_part = tokens_product(logit_grad, query)
                value_part = tokens_product(weights.astype(BF16), grad_low[rows, columns])
                for other in range(step + 1):
                    piece = slice(other * block, (other + 1) * block)
                    add(key_grads, other, key_part[piece])
                    add(value_grads, other, value_part[piece])
        for step in range(blocks):
            rows = slice(step * block, (step + 1) * block)
            cosine = table_ref[rows, :SLOT]
            sine = table_ref[rows, SLOT:]

            def unrotated(value):
                return (value * cosine - pltpu.roll(value, SLOT // 2, 1) * sine).astype(BF16)

            parts = [unrotated(query_grads[head][step] * SCALING) for head in range(GROUP)]
            parts.append(unrotated(key_grads[step] * (1.0 / LOG2E)))
            parts.append(value_grads[step].astype(BF16))
            out_ref[rows, group * JOINED : (group + 1) * JOINED] = product(
                jnp.concatenate(parts, axis=1), back_ref[...]
            ).astype(BF16)


def attention_forward(member, value, weights, table, start, heads):
    length, width = value.shape
    out_width = PAIR * GROUP * HEAD_DIM
    steps = heads.shape[0] // out_width
    kept_width = PAIR * SLOTS * SLOT
    place = jnp.asarray(placement(SLOTS), BF16)
    back = jnp.asarray(placement(PAIR * GROUP).T, BF16)
    block = min(256, length)
    whole = lambda s, m: (0, 0)
    return pl.pallas_call(
        functools.partial(forward_kernel, block),
        grid_spec=pltpu.PrefetchScalarGridSpec(
            num_scalar_prefetch=1,
            grid=(steps,),
            in_specs=[
                pl.BlockSpec((length, width), whole),
                pl.BlockSpec((width, PAIR * JOINED), lambda s, m: (0, m[0] * steps + s)),
                pl.BlockSpec((length, 2 * SLOT), whole),
                pl.BlockSpec((length, 1), whole),
                pl.BlockSpec(place.shape, whole),
                pl.BlockSpec(back.shape, whole),
                pl.BlockSpec((out_width, width), lambda s, m: (s, 0)),
            ],
            out_specs=[
                pl.BlockSpec((length, out_width), lambda s, m: (0, s)),
                pl.BlockSpec((length, kept_width), lambda s, m: (0, s)),
                pl.BlockSpec((1, length, SLOT), lambda s, m: (s, 0, 0)),
                pl.BlockSpec((length, width), whole),
            ],
            scratch_shapes=[pltpu.VMEM((length, width), F32)],
        ),
        out_shape=[
            jax.ShapeDtypeStruct((length, steps * out_width), BF16),
            jax.ShapeDtypeStruct((length, steps * kept_width), BF16),
            jax.ShapeDtypeStruct((steps, length, SLOT), F32),
            jax.ShapeDtypeStruct((length, width), BF16),
        ],
        compiler_params=pltpu.CompilerParams(vmem_limit_bytes=VMEM_LIMIT),
        cost_estimate=SMALL_COST,
        name="attention_forward",
    )(member, value, weights, table, start, place, back, heads)


def attention_backward(kept, table, start, logsum, att, branch, heads, first, steps):
    length = att.shape[0]
    out_width = PAIR * GROUP * HEAD_DIM
    kept_width = PAIR * SLOTS * SLOT
    place = jnp.asarray(placement(PAIR * GROUP), BF16)
    back = jnp.asarray(placement(SLOTS).T, BF16)
    block = min(256, length)
    flops = steps * PAIR * GROUP * length * (length // 2 + block // 2) * SLOT * 10
    return pl.pallas_call(
        functools.partial(backward_kernel, block),
        grid=(steps,),
        in_specs=[
            pl.BlockSpec((length, kept_width), lambda s: (0, s + first)),
            pl.BlockSpec((length, 2 * SLOT), lambda s: (0, 0)),
            pl.BlockSpec((length, 1), lambda s: (0, 0)),
            pl.BlockSpec((1, length, SLOT), lambda s: (s + first, 0, 0)),
            pl.BlockSpec((length, out_width), lambda s: (0, s + first)),
            pl.BlockSpec(branch.shape, lambda s: (0, 0)),
            pl.BlockSpec((out_width, branch.shape[1]), lambda s: (s + first, 0)),
            pl.BlockSpec(place.shape, lambda s: (0, 0)),
            pl.BlockSpec(back.shape, lambda s: (0, 0)),
        ],
        out_specs=pl.BlockSpec((length, PAIR * JOINED), lambda s: (0, s)),
        out_shape=jax.ShapeDtypeStruct((length, steps * PAIR * JOINED), BF16),
        compiler_params=pltpu.CompilerParams(vmem_limit_bytes=VMEM_LIMIT),
        cost_estimate=SMALL_COST,
        name="attention_backward",
    )(kept, table, start, logsum, att, branch, heads, place, back)


def fetched(parts, c_refs, c_ref, sems):
    step = pl.program_id(0)

    def copies(index):
        ref_index = sum(sum(rows) for rows in parts[:index])
        number = 0
        for block, count in enumerate(parts[index]):
            column = 0
            for ref in c_refs[ref_index : ref_index + count]:
                own, size = ref.shape
                target = c_ref.at[index % 2, pl.ds(block * own, own), pl.ds(column, size)]
                yield pltpu.make_async_copy(ref, target, sems.at[index % 2, number])
                column += size
                number += 1
            ref_index += count

    for index in range(len(parts)):

        @pl.when(step == index)
        def _():
            if index == 0:
                for copy in copies(0):
                    copy.start()
            if index + 1 < len(parts):
                for copy in copies(index + 1):
                    copy.start()
            for copy in copies(index):
                copy.wait()

    return c_ref[step % 2]


def counted(c):
    parts = tuple(tuple(len(block) for block in step) for step in c)
    return parts, [part for step in c for block in step for part in block]


def feed_kernel(parts, residual, fresh, places_ref, *refs):
    number = sum(sum(rows) for rows in parts)
    c_refs, refs = refs[:number], refs[number:]
    (dy_ref, expand_ref, down_ref), refs = refs[:3], refs[3:]
    if residual:
        hidden_ref, refs = refs[0], refs[1:]
    if not fresh:
        refs = refs[2:]
    out_ref, terms_ref, dc_ref, c_buffer, sems = refs
    hidden = down_ref.shape[0]
    c = fetched(parts, c_refs, c_buffer, sems)
    gate = product(c, expand_ref[:, :hidden])
    up = product(c, expand_ref[:, hidden:])
    dm = against(dy_ref[0], down_ref[...])
    sigmoid = jax.nn.sigmoid(gate)
    active = gate * sigmoid
    mixed = (active * up).astype(BF16)
    dgate = (dm * up * sigmoid * (1.0 + gate * (1.0 - sigmoid))).astype(BF16)
    dup = (dm * active).astype(BF16)
    terms_ref[0, 0] = mixed
    terms_ref[0, 1] = dgate
    terms_ref[0, 2] = dup
    dc = against(dgate, expand_ref[:, :hidden]) + against(dup, expand_ref[:, hidden:])
    dc_ref[0] = dc.astype(BF16)
    out = product(mixed, down_ref[...])
    if residual:
        out_ref[0] = (out + jnp.where(pl.program_id(0) == 0, hidden_ref[...], 0.0)).astype(BF16)
    else:
        out_ref[0] = out.astype(BF16)


def c_scratch(parts, rows, width):
    number = max(sum(counts) for counts in parts)
    return [pltpu.VMEM((2, rows, width), BF16), pltpu.SemaphoreType.DMA((2, number))]


def feed_forward(places, c, dy, expand, down, blocks, before=None, hidden_res=None):
    parts, flat = counted([[block] for block in c])
    steps = len(c)
    own, width = dy.shape[1] // (blocks // 4), dy.shape[2]
    hidden = down.shape[0]
    residual = hidden_res is not None
    fresh = before is None
    single = pl.Buffered(1)
    whole = lambda s, p: (0, 0)
    token = pl.BlockSpec((1, own, width), lambda s, p: (p[s, 1], p[s, 2], 0))
    operands = [places, *flat, dy, expand, down]
    in_specs = [pl.BlockSpec(memory_space=pl.ANY)] * len(flat) + [
        token,
        pl.BlockSpec(expand.shape, whole, pipeline_mode=single),
        pl.BlockSpec(down.shape, whole, pipeline_mode=single),
    ]
    if residual:
        operands.append(hidden_res)
        in_specs.append(pl.BlockSpec((own, width), whole, pipeline_mode=single))
    aliases = {}
    if not fresh:
        aliases = {len(operands): 0, len(operands) + 1: 1}
        operands += list(before)
        in_specs += [pl.BlockSpec(memory_space=pl.ANY)] * 2
    return pl.pallas_call(
        functools.partial(feed_kernel, parts, residual, fresh),
        grid_spec=pltpu.PrefetchScalarGridSpec(
            num_scalar_prefetch=1,
            grid=(steps,),
            in_specs=in_specs,
            out_specs=[
                token,
                pl.BlockSpec((1, 3, own, hidden), lambda s, p: (p[s, 0], 0, 0, 0)),
                pl.BlockSpec((1, own, width), lambda s, p: (s, 0, 0)),
            ],
            scratch_shapes=c_scratch(parts, own, width),
        ),
        out_shape=[
            jax.ShapeDtypeStruct(dy.shape, BF16),
            jax.ShapeDtypeStruct((blocks, 3, own, hidden), BF16),
            jax.ShapeDtypeStruct((steps, own, width), BF16),
        ],
        input_output_aliases=aliases,
        compiler_params=pltpu.CompilerParams(vmem_limit_bytes=VMEM_LIMIT),
        cost_estimate=SMALL_COST,
        name="feed_forward",
    )(*operands)


def accumulate(total_ref, value, columns=slice(None)):
    @pl.when(pl.program_id(0) == 0)
    def _():
        total_ref[:, columns] = value

    @pl.when(pl.program_id(0) > 0)
    def _():
        total_ref[:, columns] += value


def down_grad_kernel(rows, count, places_ref, *refs):
    dy_refs, (mixed_ref, out_ref, total_ref, dy_buffer) = refs[:count], refs[count:]
    own, hidden = mixed_ref.shape[2], mixed_ref.shape[3]
    for index in range(count):
        dy_buffer[index * own : (index + 1) * own, :] = dy_refs[index][0]
    mixed = mixed_ref[...].reshape(count * own, hidden)
    accumulate(total_ref, tokens_product(mixed, dy_buffer[...]))
    width, columns = total_ref.shape[1], out_ref.shape[2]

    @pl.when(pl.program_id(0) == pl.num_programs(0) - 1)
    def _():
        for place in range(out_ref.shape[0]):
            for to_row, size_row, to_column, row, column, size in pack_chunks(rows, width, columns):
                first = place * rows + row
                out_ref[place, to_row : to_row + size_row, to_column : to_column + size] = (
                    total_ref[first : first + size_row, column : column + size].astype(BF16)
                )


def expand_grad_kernel(parts, *refs):
    number = sum(sum(rows) for rows in parts)
    c_refs, refs = refs[:number], refs[number:]
    dgate_ref, dup_ref, _, out_ref, total_ref, c_buffer, sems = refs
    count, _, own, hidden = dgate_ref.shape
    c = fetched(parts, c_refs, c_buffer, sems)
    dgate = dgate_ref[...].reshape(count * own, hidden)
    dup = dup_ref[...].reshape(count * own, hidden)
    accumulate(total_ref, tokens_product(c, dgate), slice(0, hidden))
    accumulate(total_ref, tokens_product(c, dup), slice(hidden, None))

    @pl.when(pl.program_id(0) == pl.num_programs(0) - 1)
    def _():
        out_ref[...] = total_ref[...].astype(BF16).reshape(out_ref.shape)


def down_grads(places, dy, terms, n_dp, rows_before):
    blocks, _, own, hidden = terms.shape
    count = blocks // 4
    width = dy.shape[2]
    packed = hidden * width // (2 * hidden) // n_dp

    def dy_spec(index):
        return pl.BlockSpec((1, own, width), lambda s, p: (p[s, 0], p[s, 1] ^ index, 0))

    return pl.pallas_call(
        functools.partial(down_grad_kernel, hidden // n_dp, count),
        grid_spec=pltpu.PrefetchScalarGridSpec(
            num_scalar_prefetch=1,
            grid=(4,),
            in_specs=[dy_spec(index) for index in range(count)]
            + [pl.BlockSpec((count, 1, own, hidden), lambda s, p: (s, 0, 0, 0))],
            out_specs=pl.BlockSpec(
                (n_dp, packed, 2 * hidden),
                lambda s, p: (0, rows_before // packed, 0),
                pipeline_mode=pl.Buffered(1),
            ),
            scratch_shapes=[
                pltpu.VMEM((hidden, width), F32), pltpu.VMEM((count * own, width), BF16)
            ],
        ),
        out_shape=jax.ShapeDtypeStruct((n_dp, rows_before + packed, 2 * hidden), BF16),
        compiler_params=pltpu.CompilerParams(vmem_limit_bytes=VMEM_LIMIT),
        cost_estimate=SMALL_COST,
        name="down_grads",
    )(places, *([dy] * count), terms)


def expand_grads(c, terms, packed, rows):
    parts, flat = counted(c)
    blocks, _, own, hidden = terms.shape
    count = blocks // 4
    n_dp = packed.shape[0]
    width = n_dp * rows
    return pl.pallas_call(
        functools.partial(expand_grad_kernel, parts),
        grid=(4,),
        in_specs=[pl.BlockSpec(memory_space=pl.ANY)] * len(flat)
        + [
            pl.BlockSpec((count, 1, own, hidden), lambda s: (s, 1, 0, 0)),
            pl.BlockSpec((count, 1, own, hidden), lambda s: (s, 2, 0, 0)),
            pl.BlockSpec(memory_space=pl.ANY),
        ],
        out_specs=pl.BlockSpec(
            (n_dp, rows, 2 * hidden), lambda s: (0, 0, 0), pipeline_mode=pl.Buffered(1)
        ),
        scratch_shapes=[pltpu.VMEM((width, 2 * hidden), F32)]
        + c_scratch(parts, count * own, width),
        out_shape=jax.ShapeDtypeStruct(packed.shape, BF16),
        input_output_aliases={len(flat) + 2: 0},
        compiler_params=pltpu.CompilerParams(vmem_limit_bytes=VMEM_LIMIT),
        cost_estimate=SMALL_COST,
        name="expand_grads",
    )(*flat, terms, terms, packed)


def local(
    inputs,
    doc_ids,
    cotangent,
    attend_in,
    attend_out,
    gains,
    expand,
    contract,
    attend_in_first,
    attend_in_second,
    attend_out_first,
    attend_out_second,
    gains_first,
    gains_second,
    expand_first,
    expand_second,
    contract_first,
    contract_second,
):
    batches, rows_local, width = inputs.shape
    n_tp = lax.axis_size("tp")
    n_dp = lax.axis_size("dp")
    me = lax.axis_index("tp")
    stream_place = lax.axis_index(("hi", "lo")).astype(jnp.int32)
    stream = rows_local * batches * n_tp
    own = stream // n_tp
    qwidth = HEADS * HEAD_DIM
    kwidth = KV_HEADS * HEAD_DIM
    joined_width = qwidth + 2 * kwidth
    part_in = joined_width // n_tp
    part_out = width // n_tp
    row_in = attend_in.shape[0]
    row_down = contract.shape[0]

    def to_groups(value):
        rows = value.shape[0]
        return jnp.concatenate(
            [
                value[:, :qwidth].reshape(rows, KV_HEADS, -1),
                value[:, qwidth : qwidth + kwidth].reshape(rows, KV_HEADS, -1),
                value[:, qwidth + kwidth :].reshape(rows, KV_HEADS, -1),
            ],
            axis=2,
        ).reshape(rows, joined_width)

    def from_groups(value):
        rows = value.shape[0]
        grid = value.reshape(rows, KV_HEADS, JOINED)
        first, second = GROUP * HEAD_DIM, (GROUP + 1) * HEAD_DIM
        return jnp.concatenate(
            [
                grid[:, :, :first].reshape(rows, qwidth),
                grid[:, :, first:second].reshape(rows, kwidth),
                grid[:, :, second:].reshape(rows, kwidth),
            ],
            axis=1,
        )

    gain_columns = jnp.concatenate([gains.T, jnp.zeros((row_in, SLOT - 2), F32)], axis=1)
    attend_shard = jnp.concatenate([to_groups(attend_in), gain_columns, attend_out], axis=1)
    attend_all = lax.all_gather(
        attend_shard.astype(BF16), ("dp", "hi", "lo", "tp"), axis=0, tiled=True
    )

    n_ctx = 4 * n_tp
    expand_parts = expand.astype(BF16).reshape(row_in, 2, n_dp, n_ctx, row_down)
    expand_parts = expand_parts.transpose(3, 0, 1, 2, 4).reshape(n_ctx, row_in, -1)
    expand_shard = ctx_swap(expand_parts).reshape(n_ctx * row_in, -1)
    hidden_two = expand_shard.shape[1]
    rows_expand = n_ctx * row_in
    feed_shard = jnp.concatenate(
        [expand_shard, packed_rows(contract.astype(BF16), hidden_two)], axis=0
    )
    feed_all, feed_pieces = dp_gather(after(feed_shard, attend_all))
    expand_all = feed_all[:, :rows_expand].reshape(width, hidden_two)
    down_all = unpacked_rows(feed_all[:, rows_expand:], row_down, width).reshape(-1, width)

    ids_wide = jnp.broadcast_to(doc_ids[:, :, None].astype(BF16), (batches, rows_local, SLOT))
    moved = to_streams(jnp.concatenate([inputs, ids_wide], axis=2)).reshape(own, width + SLOT)
    resid = moved[:, :width]
    moved_all = group_gather(moved)
    resid_all = moved_all[:, :width].astype(F32)
    ids = moved_all[:, width].astype(jnp.int32)
    dy_all = lax.all_gather(after(cotangent, moved), CTX, axis=1, tiled=True)

    start = jnp.sum((ids[None, :] < ids[:, None]).astype(jnp.int32), axis=-1)
    position = (jnp.arange(stream, dtype=jnp.int32) - start).astype(F32)
    inverse = jnp.power(ROPE_BASE, -2.0 * jnp.arange(HALF, dtype=F32) / HEAD_DIM)
    angles = position[:, None] * inverse
    cosine = jnp.cos(angles)
    sine = jnp.sin(angles)
    gap = jnp.zeros((stream, SLOT // 2 - HALF), F32)
    table = jnp.concatenate([cosine, gap, cosine, gap, -sine, gap, sine, gap], axis=-1)
    start = start[:, None]

    in_low = lax.dynamic_slice(attend_all, (0, me * part_in), (width, part_in))
    gain_one = attend_all[:, joined_width].astype(F32)
    gain_two = attend_all[:, joined_width + 1].astype(F32)
    out_low = lax.dynamic_slice(
        attend_all, (me * (qwidth // n_tp), joined_width + SLOT), (qwidth // n_tp, width)
    )

    inv_all = lax.rsqrt(jnp.mean(resid_all * resid_all, axis=-1, keepdims=True) + EPSILON)
    first_in = (resid_all * inv_all * gain_one).astype(BF16)
    att_low, kept, logsum, hidden_part = attention_forward(
        me[None].astype(jnp.int32), first_in, attend_all, table, start, out_low
    )
    hidden_part = after(hidden_part, feed_pieces[0])

    def own_sum(value):
        grid = value.reshape(n_tp, own, width)
        if n_tp != 2:
            return lax.psum_scatter(grid, "tp", scatter_dimension=0, tiled=True)[0]
        came = exchange(lax.dynamic_index_in_dim(grid, 1 - me, 0, keepdims=False), "tp")
        mine = lax.dynamic_index_in_dim(grid, me, 0, keepdims=False)
        return mine.astype(F32) + came.astype(F32)

    resid = resid.astype(F32)
    hidden_res = resid + own_sum(hidden_part)
    inv_two = lax.rsqrt(jnp.mean(hidden_res * hidden_res, axis=-1, keepdims=True) + EPSILON)
    normed_two = hidden_res * inv_two
    second_in = (normed_two * gain_two).astype(BF16)
    def place_row(relative, member):
        return jnp.stack(
            [jnp.int32(relative * n_tp + member), stream_place ^ relative, me ^ member]
        ).astype(jnp.int32)

    blocks = 4 * n_tp
    parts = [
        [relative_gather(part) for part in chip] for chip in plane_parts(second_in)
    ]

    def pieces_of(relative, member):
        return [part[member] for part in parts[relative]]

    def feed_call(order, before=None, residual=None):
        rows = jnp.stack([place_row(relative, member) for relative, member in order])
        c = [pieces_of(relative, member) for relative, member in order]
        return feed_forward(rows, c, dy_all, expand_all, down_all, blocks, before, residual)

    def after_calls(*ready):
        return lax.optimization_barrier((out_all, terms) + ready)[:2]

    members = list(range(n_tp))
    far_order = [(r, member) for member in members[1:] for r in (3, 1, 2)]
    out_all, terms, first_dc = feed_call(far_order)
    out_all, terms, corner_dc = feed_call([(3, 0)], (out_all, terms))
    first_dc = first_dc.reshape(n_tp - 1, 3, own, width)
    first_came = list(first_dc)
    if n_tp == 2:
        first_came = [exchange(first_dc[0], "tp")]
    corner = relative_sum([corner_dc[0]] + [value[0] for value in first_came], n_tp == 2).astype(BF16)
    middle = width // 2
    corner = (corner[:, :middle], corner[:, middle:])
    corner_left = exchange(corner[0], "lo")
    corner_right = exchange(corner[1], "hi")
    out_all, terms, second_dc = feed_call([(1, 0), (2, 0)], after_calls(*corner))
    beside, across = relative_sum(
        [second_dc] + [value[1:] for value in first_came], n_tp == 2
    ).astype(BF16)
    left_sent = jnp.stack(
        [beside[:, :middle], total_of([beside[:, middle:], corner_right])]
    ).astype(BF16)
    right_sent = jnp.stack(
        [across[:, middle:], total_of([across[:, :middle], corner_left])]
    ).astype(BF16)
    out_all, terms, near_dc = feed_call(
        [(0, member) for member in members], after_calls(left_sent, right_sent), hidden_res
    )
    near = relative_sum([near_dc[member] for member in members])
    chip_rows = jnp.stack([place_row(relative, 0)[1:] for relative in range(4)])
    packed = down_grads(chip_rows, dy_all, terms, n_dp, rows_expand)
    left_came = after(exchange(left_sent, "lo"), packed)
    right_came = after(exchange(right_sent, "hi"), packed)
    feed_terms = expand_grads(
        [[pieces_of(relative, member) for member in members] for relative in range(4)],
        terms,
        after(packed, left_came, right_came),
        rows_expand,
    )
    left_came, right_came = after(left_came, feed_terms), after(right_came, feed_terms)
    second_grad = near.astype(F32) + jnp.concatenate(
        [total_of([left_came[0], right_came[1]]), total_of([left_came[1], right_came[0]])], axis=1
    )
    block_out = lax.psum_scatter(out_all, CTX, scatter_dimension=1, tiled=True)
    feed_sum = lax.psum_scatter(feed_terms, "dp", scatter_dimension=0, tiled=True)[0]

    upstream = lax.dynamic_slice(dy_all, (stream_place, me * own, 0), (1, own, width))[0]
    upstream = upstream.astype(F32)
    hidden_grad = upstream + norm_back(second_grad, normed_two, inv_two, gain_two)
    branch_all = group_gather(hidden_grad.astype(BF16))
    att_steps = logsum.shape[0]
    cuts = [0, att_steps // 2, att_steps] if att_steps > 1 else [0, 1]
    def plane_stage(terms, name):
        return axis_sum(terms, name, 1 if name == "hi" else 2)

    def plane_grid(value):
        return [value.reshape(n_dp, 2, 2, n_tp * row_in, -1)]

    def plane_terms(value, order):
        return plane_stage(plane_stage(plane_grid(value), order[0]), order[1])

    orders = (("hi", "lo"), ("lo", "hi"))

    def heads_back(index, branch):
        begin, end = cuts[index], cuts[index + 1]
        return attention_backward(
            kept, table, start, logsum, att_low, branch, out_low, begin, end - begin
        )

    joined_parts = [heads_back(0, branch_all)]
    in_parts = [tokens_product(first_in, joined_parts[0]).astype(BF16)]

    branch_late = after(branch_all, joined_parts[0])
    if n_tp == 2:
        heads_rows = qwidth // n_tp

        def out_columns(member):
            part = lax.dynamic_slice_in_dim(branch_late, member * part_out, part_out, 1)
            return tokens_product(att_low, part).astype(BF16)

        out_came = exchange(out_columns(1 - me), "tp")
        out_term = jnp.zeros((qwidth, part_out), BF16)
        out_term = lax.dynamic_update_slice_in_dim(out_term, out_columns(me), me * heads_rows, 0)
        out_term = lax.dynamic_update_slice_in_dim(out_term, out_came, (1 - me) * heads_rows, 0)
    else:
        out_term = tokens_product(att_low, branch_late).astype(BF16)
        out_term = out_term.reshape(qwidth // n_tp, n_tp, part_out).transpose(1, 0, 2)
        out_term = group_swap(out_term).reshape(qwidth, part_out)
    half = part_out // 2
    out_parts = [out_term[:, :half], out_term[:, half:]]

    if len(cuts) > 2:
        joined_parts.append(heads_back(1, after(branch_all, in_parts[0], out_term)))
    in_terms = [plane_stage(plane_grid(in_parts[0]), orders[0][0])]
    out_terms = [
        plane_stage(plane_grid(part), order[0]) for part, order in zip(out_parts, orders)
    ]
    came = [terms[-1] for terms in out_terms]
    came = [after(value, joined_parts[-1]) for value in came]
    for terms, value in zip(out_terms, came):
        terms[-1] = value
    if len(cuts) > 2:
        late_in = after(first_in, *came)
        in_parts.append(tokens_product(late_in, joined_parts[1]).astype(BF16))
        in_terms.append(plane_stage(plane_grid(in_parts[1]), orders[1][0]))
    late = in_terms[-1][-1]
    for terms in out_terms:
        terms[-1] = after(terms[-1], late)
    in_terms[0][-1] = after(in_terms[0][-1], late)
    feed_sum = after(feed_sum, late)
    in_terms = [plane_stage(terms, order[1]) for terms, order in zip(in_terms, orders)]
    out_terms = [plane_stage(terms, order[1]) for terms, order in zip(out_terms, orders)]
    joined_all = after(jnp.concatenate(joined_parts, axis=1), in_parts[-1])
    first_part = against(joined_all, in_low).astype(BF16)

    ready = (first_part,) + tuple(terms[-1] for terms in in_terms)
    low = F32 if n_tp != 2 else BF16

    rows = column_sum(in_terms + out_terms).reshape(n_tp, row_in, -1)
    rows = group_swap(rows.astype(low)).astype(F32).transpose(1, 0, 2)
    in_sum = rows[:, :, :part_in].reshape(row_in, joined_width)
    out_sum = rows[:, :, part_in:].reshape(row_in, width)
    expand_rows = feed_sum[:rows_expand].reshape(n_ctx, row_in, -1)
    expand_sum = ctx_swap(expand_rows).reshape(n_ctx, row_in, 2, n_dp, row_down)
    expand_sum = expand_sum.transpose(1, 2, 3, 0, 4).reshape(row_in, 2 * FF).astype(F32)
    contract_sum = unpacked_rows(feed_sum[rows_expand:].astype(F32), row_down, width)

    inv_one = lax.rsqrt(jnp.mean(resid * resid, axis=-1, keepdims=True) + EPSILON)
    first_grad = own_sum(first_part)
    first_grad = after(first_grad, *ready[1:])
    resid_grad = hidden_grad + norm_back(first_grad, resid * inv_one, inv_one, gain_one)
    shape = (batches, rows_local, width)
    grad_inputs = from_streams(resid_grad.astype(BF16).reshape(shape))

    in_sum = from_groups(in_sum)
    low_gains = gains.astype(BF16).astype(F32)
    gain_sum = jnp.stack(
        [
            jnp.sum(in_sum * attend_in.astype(BF16).astype(F32), axis=1),
            jnp.sum(expand_sum * expand.astype(BF16).astype(F32), axis=1),
        ]
    ) / low_gains

    out_fan = max(1, HEADS * HEAD_DIM // (stream // 8))
    new_in = adamw(attend_in, attend_in_first, attend_in_second, in_sum, RATE / math.sqrt(D))
    new_out = adamw(
        attend_out, attend_out_first, attend_out_second, out_sum, RATE / math.sqrt(out_fan)
    )
    new_gain = adamw(gains, gains_first, gains_second, gain_sum, GAIN_RATE)
    new_expand = adamw(expand, expand_first, expand_second, expand_sum, RATE / math.sqrt(D))
    new_contract = adamw(
        contract, contract_first, contract_second, contract_sum, RATE / math.sqrt(FF)
    )
    return (block_out, grad_inputs, *new_in, *new_out, *new_gain, *new_expand, *new_contract)


def solution(mesh):
    n_dp, n_ctx = mesh.shape["dp"], mesh.shape["ctx"]
    cut = jax.sharding.Mesh(
        mesh.devices.reshape(n_dp, 2, 2, n_ctx // 4), ("dp", "hi", "lo", "tp")
    )
    every = ("dp", "hi", "lo", "tp")
    rows = P(every, None)
    columns = P(None, every)
    tokens = P(None, every, None)
    return jax.shard_map(
        local,
        mesh=cut,
        in_specs=(tokens, columns, tokens, rows, rows, columns, rows, rows)
        + (rows,) * 4
        + (columns,) * 2
        + (rows,) * 4,
        out_specs=(tokens, tokens) + (rows,) * 6 + (columns,) * 3 + (rows,) * 6,
        check_vma=False,
    )
```

```python
import functools
import math

import jax
import jax.numpy as jnp
import numpy as np
from jax import lax
from jax.experimental import pallas as pl
from jax.experimental.pallas import tpu as pltpu
from jax.sharding import PartitionSpec as P

D = 1536
HEADS = 16
KV_HEADS = 8
HEAD_DIM = 96
FF = 4096
STEP = 10

EPSILON = 1e-06
ROPE_BASE = 100000.0
BETA_ONE = 0.9
BETA_TWO = 0.95
ADAM_EPSILON = 1e-08
DECAY = 0.1
RATE = 0.3
GAIN_RATE = 0.25

HALF = HEAD_DIM // 2
SLOT = 128
SCALING = HEAD_DIM ** (-0.5)
LOG2E = math.log2(math.e)
VMEM_LIMIT = 60 * 1024 * 1024
BF16 = jnp.bfloat16
F32 = jnp.float32
SMALL_COST = pl.CostEstimate(flops=1 << 20, bytes_accessed=1 << 20, transcendentals=0)


def against(left, right):
    return lax.dot_general(left, right, (((1,), (1,)), ((), ())), preferred_element_type=F32)


def tokens_product(left, right):
    return lax.dot_general(left, right, (((0,), (0,)), ((), ())), preferred_element_type=F32)


def product(left, right):
    return jnp.dot(left, right, preferred_element_type=F32)


def adamw(weight, first, second, grad, rate):
    first_new = BETA_ONE * first + (1.0 - BETA_ONE) * grad
    second_new = BETA_TWO * second + (1.0 - BETA_TWO) * grad * grad
    ratio = (
        first_new
        / (1.0 - BETA_ONE**STEP)
        / (jnp.sqrt(second_new / (1.0 - BETA_TWO**STEP)) + ADAM_EPSILON)
    )
    return (weight - rate * (ratio + DECAY * weight), first_new, second_new)


def norm_back(grad_in, normed, inverse, gain):
    scaled = grad_in * gain
    return inverse * (scaled - normed * jnp.mean(scaled * normed, axis=-1, keepdims=True))


def exchange(value, axis, bit=1):
    count = lax.axis_size(axis)
    return lax.ppermute(value, axis, [(i, i ^ bit) for i in range(count)])


def shifted(value, step):
    count = lax.axis_size("dp")
    return lax.ppermute(value, "dp", [(i, (i + step) % count) for i in range(count)])


def total_of(terms):
    total = terms[0].astype(F32)
    for term in terms[1:]:
        total = total + term.astype(F32)
    return total


def taken(value, index, axis):
    return lax.dynamic_index_in_dim(value, index, axis, keepdims=True)


def axis_sum(terms, name, axis):
    mine = lax.axis_index(name)
    sent = total_of([taken(term, 1 - mine, axis) for term in terms]).astype(BF16)
    came = exchange(sent, name)
    return [taken(term, mine, axis) for term in terms] + [came]


def dp_sum(value, *ready):
    came = lax.all_to_all(value, "dp", split_axis=0, concat_axis=0, tiled=True)
    if ready:
        came = after(came, *ready)
    return jnp.sum(came.astype(F32), axis=0)


def column_sum(groups, *ready):
    sums = [total_of(terms).astype(BF16) for terms in groups]
    sums = [one.reshape(one.shape[:1] + one.shape[-2:]) for one in sums]
    return dp_sum(jnp.concatenate(sums, axis=2), *ready)


def after(value, *others):
    return lax.optimization_barrier((value,) + others)[0]


def put(whole, piece, *places):
    index = places + (0,) * (whole.ndim - len(places))
    return lax.dynamic_update_slice(whole, piece.reshape((1,) * len(places) + piece.shape), index)


def dp_gather(shard):
    n_dp = lax.axis_size("dp")
    place = lax.axis_index("dp")
    column = put(jnp.zeros((n_dp,) + shard.shape, shard.dtype), shard, place)
    pieces = [shifted(shard, step) for step in range(1, n_dp)]
    for step, piece in enumerate(pieces):
        column = put(column, piece, (place - step - 1) % n_dp)
    return column, pieces


def plane_parts(value):
    middle = value.shape[-1] // 2
    beside = exchange(value, "lo")
    across = exchange(value, "hi")
    corner = [exchange(beside[..., :middle], "hi"), exchange(across[..., middle:], "lo")]
    return [[value], [beside], [across], corner]


def pack_chunks(rows, width, columns):
    full, rest = divmod(width, columns)
    chunks = [(index * rows, rows, 0, 0, index * columns, columns) for index in range(full)]
    if rest:
        count = columns // rest
        part = rows // count
        chunks += [
            (full * rows, part, index * rest, index * part, full * columns, rest)
            for index in range(count)
        ]
    return chunks


def packed_rows(value, columns):
    rows, width = value.shape
    packed = jnp.zeros((rows * width // columns, columns), value.dtype)
    for to_row, count, to_column, row, column, size in pack_chunks(rows, width, columns):
        part = value[row : row + count, column : column + size]
        packed = lax.dynamic_update_slice(packed, part, (to_row, to_column))
    return packed


def unpacked_rows(packed, rows, width):
    columns = packed.shape[-1]
    whole = jnp.zeros(packed.shape[:-2] + (rows, width), packed.dtype)
    lead = (0,) * (packed.ndim - 2)
    for to_row, count, to_column, row, column, size in pack_chunks(rows, width, columns):
        part = packed[..., to_row : to_row + count, to_column : to_column + size]
        whole = lax.dynamic_update_slice(whole, part, lead + (row, column))
    return whole


def relative_gather(value):
    pieces = [value]
    bit = 1
    while bit < lax.axis_size("tp"):
        pieces = pieces + [exchange(piece, "tp", bit) for piece in pieces]
        bit *= 2
    return pieces


def relative_sum(pieces, arrived=False):
    pieces = list(pieces)
    if arrived:
        return total_of(pieces)
    bit = len(pieces) // 2
    while bit:
        for index in range(bit):
            came = exchange(pieces[index + bit].astype(BF16), "tp", bit)
            pieces[index] = pieces[index].astype(F32) + came.astype(F32)
        bit //= 2
    return pieces[0]


def group_gather(value):
    if lax.axis_size("tp") != 2:
        return lax.all_gather(value, "tp", axis=0, tiled=True)
    came = exchange(value, "tp")
    first = lax.axis_index("tp") == 0
    return jnp.concatenate([jnp.where(first, value, came), jnp.where(first, came, value)], axis=0)


def group_swap(value):
    if lax.axis_size("tp") != 2:
        return lax.all_to_all(value, "tp", split_axis=0, concat_axis=0, tiled=True)
    me = lax.axis_index("tp")
    mine = taken(value, me, 0)
    came = exchange(taken(value, 1 - me, 0), "tp")
    return jnp.concatenate([jnp.where(me == 0, mine, came), jnp.where(me == 0, came, mine)], axis=0)


CTX = ("hi", "lo", "tp")


def ctx_swap(value):
    return lax.all_to_all(value, CTX, split_axis=0, concat_axis=0, tiled=True)


def stream_moves(batches):
    group = lax.axis_size("tp")
    count = batches * group
    return [
        [(i, group * ((i + step) % batches) + i // batches) for i in range(count)]
        for step in range(batches)
    ]


def to_streams(value):
    batches = value.shape[0]
    me = lax.axis_index(CTX)
    stream = me // lax.axis_size("tp")
    whole = jnp.zeros_like(value)
    for step, pairs in enumerate(stream_moves(batches)):
        piece = lax.ppermute(taken(value, (me + step) % batches, 0), CTX, pairs)
        whole = lax.dynamic_update_slice_in_dim(whole, piece, (stream - step) % batches, 0)
    return whole


def from_streams(value):
    batches = value.shape[0]
    me = lax.axis_index(CTX)
    stream = me // lax.axis_size("tp")
    whole = jnp.zeros_like(value)
    for step, pairs in enumerate(stream_moves(batches)):
        back = [(b, a) for a, b in pairs]
        piece = lax.ppermute(taken(value, (stream - step) % batches, 0), CTX, back)
        whole = lax.dynamic_update_slice_in_dim(whole, piece, (me + step) % batches, 0)
    return whole


GROUP = HEADS // KV_HEADS
SLOTS = GROUP + 2
JOINED = SLOTS * HEAD_DIM
PAIR = 2


def placement(slots):
    matrix = np.zeros((slots * HEAD_DIM, slots * SLOT), np.float32)
    for slot in range(slots):
        for half in range(2):
            for m in range(HALF):
                matrix[slot * HEAD_DIM + half * HALF + m, slot * SLOT + half * (SLOT // 2) + m] = 1
    return matrix


def mask_of(start, first_row, rows, keys):
    row = first_row + lax.broadcasted_iota(jnp.int32, (rows, keys), 0)
    column = lax.broadcasted_iota(jnp.int32, (rows, keys), 1)
    return (column >= start) & (column <= row)


def columns_of(group, slot):
    first = (group * SLOTS + slot) * SLOT
    return slice(first, first + SLOT)


def forward_kernel(block, member_ref, input_ref, weight_ref, table_ref, start_ref, place_ref,
                   back_ref, head_ref, out_ref, kept_ref, logsum_ref, part_ref, total_ref):
    length = input_ref.shape[0]
    cosine = table_ref[:, :SLOT]
    sine = table_ref[:, SLOT:]
    for group in range(PAIR):
        weight = weight_ref[:, group * JOINED : (group + 1) * JOINED]
        joined = product(input_ref[...], weight).astype(BF16)
        placed = product(joined, place_ref[...])
        for slot in range(SLOTS):
            part = placed[:, slot * SLOT : (slot + 1) * SLOT]
            if slot <= GROUP:
                part = part * cosine + pltpu.roll(part, SLOT // 2, 1) * sine
            if slot < GROUP:
                part = part * (SCALING * LOG2E)
            kept_ref[:, columns_of(group, slot)] = part.astype(BF16)
    lane = lax.broadcasted_iota(jnp.int32, (block, SLOT), 1)
    for first in range(0, length, block):
        rows = slice(first, first + block)
        count = first + block
        mask = mask_of(start_ref[rows, :], first, block, count)
        outs = []
        logsums = jnp.zeros((block, SLOT), F32)
        for group in range(PAIR):
            keys = kept_ref[:count, columns_of(group, GROUP)]
            values = kept_ref[:count, columns_of(group, GROUP + 1)]
            for head in range(GROUP):
                logits = against(kept_ref[rows, columns_of(group, head)], keys)
                logits = jnp.where(mask, logits, -1e30)
                peak = jnp.max(logits, axis=-1, keepdims=True)
                weights = jnp.exp2(logits - peak)
                total = jnp.sum(weights, axis=-1, keepdims=True)
                outs.append((product(weights.astype(BF16), values) / total).astype(BF16))
                logsums = jnp.where(
                    lane == group * GROUP + head, peak + jnp.log2(total), logsums
                )
        logsum_ref[0, rows, :] = logsums
        compact = product(jnp.concatenate(outs, axis=1), back_ref[...]).astype(BF16)
        out_ref[rows, :] = compact
        part = product(compact, head_ref[...])

        @pl.when(pl.program_id(0) == 0)
        def _():
            total_ref[rows, :] = part

        @pl.when(pl.program_id(0) > 0)
        def _():
            total_ref[rows, :] += part

    @pl.when(pl.program_id(0) == pl.num_programs(0) - 1)
    def _():
        part_ref[...] = total_ref[...].astype(BF16)


def backward_kernel(block, kept_ref, table_ref, start_ref, logsum_ref, att_ref, branch_ref,
                    head_ref, place_ref, back_ref, out_ref):
    length = kept_ref.shape[0]
    att = product(att_ref[...], place_ref[...])
    grad = product(against(branch_ref[...], head_ref[...]).astype(BF16), place_ref[...])
    both = att * grad
    grad_low = grad.astype(BF16)
    blocks = length // block

    def add(store, index, value):
        store[index] = value if store[index] is None else store[index] + value

    for group in range(PAIR):
        key_grads = [None] * blocks
        value_grads = [None] * blocks
        query_grads = [[None] * blocks for _ in range(GROUP)]
        for step in range(blocks):
            first = step * block
            rows = slice(first, first + block)
            count = first + block
            mask = mask_of(start_ref[rows, :], first, block, count)
            keys = kept_ref[:count, columns_of(group, GROUP)]
            values = kept_ref[:count, columns_of(group, GROUP + 1)]
            for head in range(GROUP):
                index = group * GROUP + head
                columns = slice(index * SLOT, (index + 1) * SLOT)
                query = kept_ref[rows, columns_of(group, head)]
                delta = jnp.sum(both[rows, columns], axis=-1, keepdims=True)
                logits = against(query, keys)
                weights = jnp.where(
                    mask, jnp.exp2(logits - logsum_ref[0, rows, index : index + 1]), 0.0
                )
                weight_grad = against(grad_low[rows, columns], values)
                logit_grad = (weights * (weight_grad - delta)).astype(BF16)
                query_grads[head][step] = product(logit_grad, keys)
                key_part = tokens_product(logit_grad, query)
                value_part = tokens_product(weights.astype(BF16), grad_low[rows, columns])
                for other in range(step + 1):
                    piece = slice(other * block, (other + 1) * block)
                    add(key_grads, other, key_part[piece])
                    add(value_grads, other, value_part[piece])
        for step in range(blocks):
            rows = slice(step * block, (step + 1) * block)
            cosine = table_ref[rows, :SLOT]
            sine = table_ref[rows, SLOT:]

            def unrotated(value):
                return (value * cosine - pltpu.roll(value, SLOT // 2, 1) * sine).astype(BF16)

            parts = [unrotated(query_grads[head][step] * SCALING) for head in range(GROUP)]
            parts.append(unrotated(key_grads[step] * (1.0 / LOG2E)))
            parts.append(value_grads[step].astype(BF16))
            out_ref[rows, group * JOINED : (group + 1) * JOINED] = product(
                jnp.concatenate(parts, axis=1), back_ref[...]
            ).astype(BF16)


def attention_forward(member, value, weights, table, start, heads):
    length, width = value.shape
    out_width = PAIR * GROUP * HEAD_DIM
    steps = heads.shape[0] // out_width
    kept_width = PAIR * SLOTS * SLOT
    place = jnp.asarray(placement(SLOTS), BF16)
    back = jnp.asarray(placement(PAIR * GROUP).T, BF16)
    block = min(256, length)
    whole = lambda s, m: (0, 0)
    return pl.pallas_call(
        functools.partial(forward_kernel, block),
        grid_spec=pltpu.PrefetchScalarGridSpec(
            num_scalar_prefetch=1,
            grid=(steps,),
            in_specs=[
                pl.BlockSpec((length, width), whole),
                pl.BlockSpec((width, PAIR * JOINED), lambda s, m: (0, m[0] * steps + s)),
                pl.BlockSpec((length, 2 * SLOT), whole),
                pl.BlockSpec((length, 1), whole),
                pl.BlockSpec(place.shape, whole),
                pl.BlockSpec(back.shape, whole),
                pl.BlockSpec((out_width, width), lambda s, m: (s, 0)),
            ],
            out_specs=[
                pl.BlockSpec((length, out_width), lambda s, m: (0, s)),
                pl.BlockSpec((length, kept_width), lambda s, m: (0, s)),
                pl.BlockSpec((1, length, SLOT), lambda s, m: (s, 0, 0)),
                pl.BlockSpec((length, width), whole),
            ],
            scratch_shapes=[pltpu.VMEM((length, width), F32)],
        ),
        out_shape=[
            jax.ShapeDtypeStruct((length, steps * out_width), BF16),
            jax.ShapeDtypeStruct((length, steps * kept_width), BF16),
            jax.ShapeDtypeStruct((steps, length, SLOT), F32),
            jax.ShapeDtypeStruct((length, width), BF16),
        ],
        compiler_params=pltpu.CompilerParams(vmem_limit_bytes=VMEM_LIMIT),
        cost_estimate=SMALL_COST,
        name="attention_forward",
    )(member, value, weights, table, start, place, back, heads)


def attention_backward(kept, table, start, logsum, att, branch, heads, first, steps):
    length = att.shape[0]
    out_width = PAIR * GROUP * HEAD_DIM
    kept_width = PAIR * SLOTS * SLOT
    place = jnp.asarray(placement(PAIR * GROUP), BF16)
    back = jnp.asarray(placement(SLOTS).T, BF16)
    block = min(256, length)
    flops = steps * PAIR * GROUP * length * (length // 2 + block // 2) * SLOT * 10
    return pl.pallas_call(
        functools.partial(backward_kernel, block),
        grid=(steps,),
        in_specs=[
            pl.BlockSpec((length, kept_width), lambda s: (0, s + first)),
            pl.BlockSpec((length, 2 * SLOT), lambda s: (0, 0)),
            pl.BlockSpec((length, 1), lambda s: (0, 0)),
            pl.BlockSpec((1, length, SLOT), lambda s: (s + first, 0, 0)),
            pl.BlockSpec((length, out_width), lambda s: (0, s + first)),
            pl.BlockSpec(branch.shape, lambda s: (0, 0)),
            pl.BlockSpec((out_width, branch.shape[1]), lambda s: (s + first, 0)),
            pl.BlockSpec(place.shape, lambda s: (0, 0)),
            pl.BlockSpec(back.shape, lambda s: (0, 0)),
        ],
        out_specs=pl.BlockSpec((length, PAIR * JOINED), lambda s: (0, s)),
        out_shape=jax.ShapeDtypeStruct((length, steps * PAIR * JOINED), BF16),
        compiler_params=pltpu.CompilerParams(vmem_limit_bytes=VMEM_LIMIT),
        cost_estimate=SMALL_COST,
        name="attention_backward",
    )(kept, table, start, logsum, att, branch, heads, place, back)


def fetched(parts, c_refs, c_ref, sems):
    step = pl.program_id(0)

    def copies(index):
        ref_index = sum(sum(rows) for rows in parts[:index])
        number = 0
        for block, count in enumerate(parts[index]):
            column = 0
            for ref in c_refs[ref_index : ref_index + count]:
                own, size = ref.shape
                target = c_ref.at[index % 2, pl.ds(block * own, own), pl.ds(column, size)]
                yield pltpu.make_async_copy(ref, target, sems.at[index % 2, number])
                column += size
                number += 1
            ref_index += count

    for index in range(len(parts)):

        @pl.when(step == index)
        def _():
            if index == 0:
                for copy in copies(0):
                    copy.start()
            if index + 1 < len(parts):
                for copy in copies(index + 1):
                    copy.start()
            for copy in copies(index):
                copy.wait()

    return c_ref[step % 2]


def counted(c):
    parts = tuple(tuple(len(block) for block in step) for step in c)
    return parts, [part for step in c for block in step for part in block]


def feed_kernel(parts, residual, fresh, places_ref, *refs):
    number = sum(sum(rows) for rows in parts)
    c_refs, refs = refs[:number], refs[number:]
    (dy_ref, expand_ref, down_ref), refs = refs[:3], refs[3:]
    if residual:
        hidden_ref, refs = refs[0], refs[1:]
    if not fresh:
        refs = refs[3:]
    out_ref, mixed_ref, both_ref, dc_ref, c_buffer, sems = refs
    hidden = down_ref.shape[0]
    c = fetched(parts, c_refs, c_buffer, sems)
    gate = product(c, expand_ref[:, :hidden])
    up = product(c, expand_ref[:, hidden:])
    dm = against(dy_ref[0], down_ref[...])
    sigmoid = jax.nn.sigmoid(gate)
    active = gate * sigmoid
    mixed = (active * up).astype(BF16)
    dgate = (dm * up * sigmoid * (1.0 + gate * (1.0 - sigmoid))).astype(BF16)
    dup = (dm * active).astype(BF16)
    mixed_ref[0] = mixed
    both_ref[0, :, :hidden] = dgate
    both_ref[0, :, hidden:] = dup
    dc = against(both_ref[0], expand_ref[...])
    dc_ref[0] = dc.astype(BF16)
    out = product(mixed, down_ref[...])
    if residual:
        out_ref[0] = (out + jnp.where(pl.program_id(0) == 0, hidden_ref[...], 0.0)).astype(BF16)
    else:
        out_ref[0] = out.astype(BF16)


def c_scratch(parts, rows, width):
    number = max(sum(counts) for counts in parts)
    return [pltpu.VMEM((2, rows, width), BF16), pltpu.SemaphoreType.DMA((2, number))]


def feed_forward(places, c, dy, expand, down, blocks, before=None, hidden_res=None):
    parts, flat = counted([[block] for block in c])
    steps = len(c)
    own, width = dy.shape[1] // (blocks // 4), dy.shape[2]
    hidden = down.shape[0]
    residual = hidden_res is not None
    fresh = before is None
    single = pl.Buffered(1)
    whole = lambda s, p: (0, 0)
    token = pl.BlockSpec((1, own, width), lambda s, p: (p[s, 1], p[s, 2], 0))
    operands = [places, *flat, dy, expand, down]
    in_specs = [pl.BlockSpec(memory_space=pl.ANY)] * len(flat) + [
        token,
        pl.BlockSpec(expand.shape, whole, pipeline_mode=single),
        pl.BlockSpec(down.shape, whole, pipeline_mode=single),
    ]
    if residual:
        operands.append(hidden_res)
        in_specs.append(pl.BlockSpec((own, width), whole, pipeline_mode=single))
    aliases = {}
    if not fresh:
        aliases = {len(operands) + index: index for index in range(3)}
        operands += list(before)
        in_specs += [pl.BlockSpec(memory_space=pl.ANY)] * 3
    return pl.pallas_call(
        functools.partial(feed_kernel, parts, residual, fresh),
        grid_spec=pltpu.PrefetchScalarGridSpec(
            num_scalar_prefetch=1,
            grid=(steps,),
            in_specs=in_specs,
            out_specs=[
                token,
                pl.BlockSpec((1, own, hidden), lambda s, p: (p[s, 0], 0, 0)),
                pl.BlockSpec((1, own, 2 * hidden), lambda s, p: (p[s, 0], 0, 0)),
                pl.BlockSpec((1, own, width), lambda s, p: (s, 0, 0)),
            ],
            scratch_shapes=c_scratch(parts, own, width),
        ),
        out_shape=[
            jax.ShapeDtypeStruct(dy.shape, BF16),
            jax.ShapeDtypeStruct((blocks, own, hidden), BF16),
            jax.ShapeDtypeStruct((blocks, own, 2 * hidden), BF16),
            jax.ShapeDtypeStruct((steps, own, width), BF16),
        ],
        input_output_aliases=aliases,
        compiler_params=pltpu.CompilerParams(vmem_limit_bytes=VMEM_LIMIT),
        cost_estimate=SMALL_COST,
        name="feed_forward",
    )(*operands)


def accumulate(total_ref, value):
    @pl.when(pl.program_id(0) == 0)
    def _():
        total_ref[...] = value

    @pl.when(pl.program_id(0) > 0)
    def _():
        total_ref[...] += value


def down_grad_kernel(rows, count, places_ref, *refs):
    dy_refs, (mixed_ref, out_ref, total_ref, dy_buffer) = refs[:count], refs[count:]
    _, own, hidden = mixed_ref.shape
    for index in range(count):
        dy_buffer[index * own : (index + 1) * own, :] = dy_refs[index][0]
    mixed = mixed_ref[...].reshape(count * own, hidden)
    accumulate(total_ref, tokens_product(mixed, dy_buffer[...]))
    width, columns = total_ref.shape[1], out_ref.shape[2]

    @pl.when(pl.program_id(0) == pl.num_programs(0) - 1)
    def _():
        for place in range(out_ref.shape[0]):
            for to_row, size_row, to_column, row, column, size in pack_chunks(rows, width, columns):
                first = place * rows + row
                out_ref[place, to_row : to_row + size_row, to_column : to_column + size] = (
                    total_ref[first : first + size_row, column : column + size].astype(BF16)
                )


def expand_grad_kernel(parts, *refs):
    number = sum(sum(rows) for rows in parts)
    c_refs, refs = refs[:number], refs[number:]
    both_ref, _, out_ref, total_ref, c_buffer, sems = refs
    count, own, hidden_two = both_ref.shape
    c = fetched(parts, c_refs, c_buffer, sems)
    accumulate(total_ref, tokens_product(c, both_ref[...].reshape(count * own, hidden_two)))

    @pl.when(pl.program_id(0) == pl.num_programs(0) - 1)
    def _():
        out_ref[...] = total_ref[...].astype(BF16).reshape(out_ref.shape)


def down_grads(places, dy, mixed, n_dp, rows_before):
    blocks, own, hidden = mixed.shape
    count = blocks // 4
    width = dy.shape[2]
    packed = hidden * width // (2 * hidden) // n_dp

    def dy_spec(index):
        return pl.BlockSpec((1, own, width), lambda s, p: (p[s, 0], p[s, 1] ^ index, 0))

    return pl.pallas_call(
        functools.partial(down_grad_kernel, hidden // n_dp, count),
        grid_spec=pltpu.PrefetchScalarGridSpec(
            num_scalar_prefetch=1,
            grid=(4,),
            in_specs=[dy_spec(index) for index in range(count)]
            + [pl.BlockSpec((count, own, hidden), lambda s, p: (s, 0, 0))],
            out_specs=pl.BlockSpec(
                (n_dp, packed, 2 * hidden),
                lambda s, p: (0, rows_before // packed, 0),
                pipeline_mode=pl.Buffered(1),
            ),
            scratch_shapes=[
                pltpu.VMEM((hidden, width), F32), pltpu.VMEM((count * own, width), BF16)
            ],
        ),
        out_shape=jax.ShapeDtypeStruct((n_dp, rows_before + packed, 2 * hidden), BF16),
        compiler_params=pltpu.CompilerParams(vmem_limit_bytes=VMEM_LIMIT),
        cost_estimate=SMALL_COST,
        name="down_grads",
    )(places, *([dy] * count), mixed)


def expand_grads(c, both, packed, rows):
    parts, flat = counted(c)
    blocks, own, hidden_two = both.shape
    count = blocks // 4
    n_dp = packed.shape[0]
    width = n_dp * rows
    return pl.pallas_call(
        functools.partial(expand_grad_kernel, parts),
        grid=(4,),
        in_specs=[pl.BlockSpec(memory_space=pl.ANY)] * len(flat)
        + [
            pl.BlockSpec((count, own, hidden_two), lambda s: (s, 0, 0)),
            pl.BlockSpec(memory_space=pl.ANY),
        ],
        out_specs=pl.BlockSpec(
            (n_dp, rows, hidden_two), lambda s: (0, 0, 0), pipeline_mode=pl.Buffered(1)
        ),
        scratch_shapes=[pltpu.VMEM((width, hidden_two), F32)]
        + c_scratch(parts, count * own, width),
        out_shape=jax.ShapeDtypeStruct(packed.shape, BF16),
        input_output_aliases={len(flat) + 1: 0},
        compiler_params=pltpu.CompilerParams(vmem_limit_bytes=VMEM_LIMIT),
        cost_estimate=SMALL_COST,
        name="expand_grads",
    )(*flat, both, packed)


def local(
    inputs,
    doc_ids,
    cotangent,
    attend_in,
    attend_out,
    gains,
    expand,
    contract,
    attend_in_first,
    attend_in_second,
    attend_out_first,
    attend_out_second,
    gains_first,
    gains_second,
    expand_first,
    expand_second,
    contract_first,
    contract_second,
):
    batches, rows_local, width = inputs.shape
    n_tp = lax.axis_size("tp")
    n_dp = lax.axis_size("dp")
    me = lax.axis_index("tp")
    stream_place = lax.axis_index(("hi", "lo")).astype(jnp.int32)
    stream = rows_local * batches * n_tp
    own = stream // n_tp
    qwidth = HEADS * HEAD_DIM
    kwidth = KV_HEADS * HEAD_DIM
    joined_width = qwidth + 2 * kwidth
    part_in = joined_width // n_tp
    part_out = width // n_tp
    row_in = attend_in.shape[0]
    row_down = contract.shape[0]

    def to_groups(value):
        rows = value.shape[0]
        return jnp.concatenate(
            [
                value[:, :qwidth].reshape(rows, KV_HEADS, -1),
                value[:, qwidth : qwidth + kwidth].reshape(rows, KV_HEADS, -1),
                value[:, qwidth + kwidth :].reshape(rows, KV_HEADS, -1),
            ],
            axis=2,
        ).reshape(rows, joined_width)

    def from_groups(value):
        rows = value.shape[0]
        grid = value.reshape(rows, KV_HEADS, JOINED)
        first, second = GROUP * HEAD_DIM, (GROUP + 1) * HEAD_DIM
        return jnp.concatenate(
            [
                grid[:, :, :first].reshape(rows, qwidth),
                grid[:, :, first:second].reshape(rows, kwidth),
                grid[:, :, second:].reshape(rows, kwidth),
            ],
            axis=1,
        )

    gain_columns = jnp.concatenate([gains.T, jnp.zeros((row_in, SLOT - 2), F32)], axis=1)
    attend_shard = jnp.concatenate([to_groups(attend_in), gain_columns, attend_out], axis=1)
    attend_all = lax.all_gather(
        attend_shard.astype(BF16), ("dp", "hi", "lo", "tp"), axis=0, tiled=True
    )

    n_ctx = 4 * n_tp
    expand_parts = expand.astype(BF16).reshape(row_in, 2, n_dp, n_ctx, row_down)
    expand_parts = expand_parts.transpose(3, 0, 1, 2, 4).reshape(n_ctx, row_in, -1)
    expand_shard = ctx_swap(expand_parts).reshape(n_ctx * row_in, -1)
    hidden_two = expand_shard.shape[1]
    rows_expand = n_ctx * row_in
    feed_shard = jnp.concatenate(
        [expand_shard, packed_rows(contract.astype(BF16), hidden_two)], axis=0
    )
    feed_all, feed_pieces = dp_gather(after(feed_shard, attend_all))
    expand_all = feed_all[:, :rows_expand].reshape(width, hidden_two)
    down_all = unpacked_rows(feed_all[:, rows_expand:], row_down, width).reshape(-1, width)

    ids_wide = jnp.broadcast_to(doc_ids[:, :, None].astype(BF16), (batches, rows_local, SLOT))
    moved = to_streams(jnp.concatenate([inputs, ids_wide], axis=2)).reshape(own, width + SLOT)
    resid = moved[:, :width]
    moved_all = group_gather(moved)
    resid_all = moved_all[:, :width].astype(F32)
    ids = moved_all[:, width].astype(jnp.int32)
    dy_all = lax.all_gather(after(cotangent, moved), CTX, axis=1, tiled=True)

    start = jnp.sum((ids[None, :] < ids[:, None]).astype(jnp.int32), axis=-1)
    position = (jnp.arange(stream, dtype=jnp.int32) - start).astype(F32)
    inverse = jnp.power(ROPE_BASE, -2.0 * jnp.arange(HALF, dtype=F32) / HEAD_DIM)
    angles = position[:, None] * inverse
    cosine = jnp.cos(angles)
    sine = jnp.sin(angles)
    gap = jnp.zeros((stream, SLOT // 2 - HALF), F32)
    table = jnp.concatenate([cosine, gap, cosine, gap, -sine, gap, sine, gap], axis=-1)
    start = start[:, None]

    in_low = lax.dynamic_slice(attend_all, (0, me * part_in), (width, part_in))
    gain_one = attend_all[:, joined_width].astype(F32)
    gain_two = attend_all[:, joined_width + 1].astype(F32)
    out_low = lax.dynamic_slice(
        attend_all, (me * (qwidth // n_tp), joined_width + SLOT), (qwidth // n_tp, width)
    )

    inv_all = lax.rsqrt(jnp.mean(resid_all * resid_all, axis=-1, keepdims=True) + EPSILON)
    first_in = (resid_all * inv_all * gain_one).astype(BF16)
    att_low, kept, logsum, hidden_part = attention_forward(
        me[None].astype(jnp.int32), first_in, attend_all, table, start, out_low
    )
    hidden_part = after(hidden_part, feed_pieces[0])

    def own_sum(value):
        grid = value.reshape(n_tp, own, width)
        if n_tp != 2:
            return lax.psum_scatter(grid, "tp", scatter_dimension=0, tiled=True)[0]
        came = exchange(lax.dynamic_index_in_dim(grid, 1 - me, 0, keepdims=False), "tp")
        mine = lax.dynamic_index_in_dim(grid, me, 0, keepdims=False)
        return mine.astype(F32) + came.astype(F32)

    resid = resid.astype(F32)
    hidden_res = resid + own_sum(hidden_part)
    inv_two = lax.rsqrt(jnp.mean(hidden_res * hidden_res, axis=-1, keepdims=True) + EPSILON)
    normed_two = hidden_res * inv_two
    second_in = (normed_two * gain_two).astype(BF16)
    def place_row(relative, member):
        return jnp.stack(
            [jnp.int32(relative * n_tp + member), stream_place ^ relative, me ^ member]
        ).astype(jnp.int32)

    blocks = 4 * n_tp
    parts = [
        [relative_gather(part) for part in chip] for chip in plane_parts(second_in)
    ]

    def pieces_of(relative, member):
        return [part[member] for part in parts[relative]]

    def feed_call(order, before=None, residual=None):
        rows = jnp.stack([place_row(relative, member) for relative, member in order])
        c = [pieces_of(relative, member) for relative, member in order]
        return feed_forward(rows, c, dy_all, expand_all, down_all, blocks, before, residual)

    def after_calls(*ready):
        return lax.optimization_barrier((out_all, mixed, both) + ready)[:3]

    members = list(range(n_tp))
    far_order = [(r, member) for member in members[1:] for r in (3, 1, 2)]
    out_all, mixed, both, first_dc = feed_call(far_order)
    out_all, mixed, both, corner_dc = feed_call([(3, 0)], (out_all, mixed, both))
    first_dc = first_dc.reshape(n_tp - 1, 3, own, width)
    first_came = list(first_dc)
    if n_tp == 2:
        first_came = [exchange(first_dc[0], "tp")]
    corner = relative_sum([corner_dc[0]] + [value[0] for value in first_came], n_tp == 2).astype(BF16)
    middle = width // 2
    corner = (corner[:, :middle], corner[:, middle:])
    corner_left = exchange(corner[0], "lo")
    corner_right = exchange(corner[1], "hi")
    out_all, mixed, both, second_dc = feed_call([(1, 0), (2, 0)], after_calls(*corner))
    beside, across = relative_sum(
        [second_dc] + [value[1:] for value in first_came], n_tp == 2
    ).astype(BF16)
    left_sent = jnp.stack(
        [beside[:, :middle], total_of([beside[:, middle:], corner_right])]
    ).astype(BF16)
    right_sent = jnp.stack(
        [across[:, middle:], total_of([across[:, :middle], corner_left])]
    ).astype(BF16)
    out_all, mixed, both, near_dc = feed_call(
        [(0, member) for member in members], after_calls(left_sent, right_sent), hidden_res
    )
    near = relative_sum([near_dc[member] for member in members])
    chip_rows = jnp.stack([place_row(relative, 0)[1:] for relative in range(4)])
    packed = down_grads(chip_rows, dy_all, mixed, n_dp, rows_expand)
    left_came = after(exchange(left_sent, "lo"), packed)
    right_came = after(exchange(right_sent, "hi"), packed)
    feed_terms = expand_grads(
        [[pieces_of(relative, member) for member in members] for relative in range(4)],
        both,
        after(packed, left_came, right_came),
        rows_expand,
    )
    left_came, right_came = after(left_came, feed_terms), after(right_came, feed_terms)
    second_grad = near.astype(F32) + jnp.concatenate(
        [total_of([left_came[0], right_came[1]]), total_of([left_came[1], right_came[0]])], axis=1
    )
    block_out = lax.psum_scatter(out_all, CTX, scatter_dimension=1, tiled=True)
    feed_sum = lax.psum_scatter(feed_terms, "dp", scatter_dimension=0, tiled=True)[0]

    upstream = lax.dynamic_slice(dy_all, (stream_place, me * own, 0), (1, own, width))[0]
    upstream = upstream.astype(F32)
    hidden_grad = upstream + norm_back(second_grad, normed_two, inv_two, gain_two)
    branch_all = group_gather(hidden_grad.astype(BF16))
    att_steps = logsum.shape[0]
    cuts = [0, att_steps // 2, att_steps] if att_steps > 1 else [0, 1]
    def plane_stage(terms, name):
        return axis_sum(terms, name, 1 if name == "hi" else 2)

    def plane_grid(value):
        return [value.reshape(n_dp, 2, 2, n_tp * row_in, -1)]

    def plane_terms(value, order):
        return plane_stage(plane_stage(plane_grid(value), order[0]), order[1])

    orders = (("hi", "lo"), ("lo", "hi"))

    def heads_back(index, branch):
        begin, end = cuts[index], cuts[index + 1]
        return attention_backward(
            kept, table, start, logsum, att_low, branch, out_low, begin, end - begin
        )

    joined_parts = [heads_back(0, branch_all)]
    in_parts = [tokens_product(first_in, joined_parts[0]).astype(BF16)]

    if len(cuts) > 2:
        joined_parts.append(heads_back(1, after(branch_all, in_parts[0])))
    in_terms = [plane_stage(plane_grid(in_parts[0]), orders[0][0])]
    if len(cuts) > 2:
        in_parts.append(tokens_product(first_in, joined_parts[1]).astype(BF16))
        in_terms.append(plane_stage(plane_grid(in_parts[1]), orders[1][0]))

    branch_late = after(branch_all, in_parts[-1])
    if n_tp == 2:
        heads_rows = qwidth // n_tp

        def out_columns(member):
            part = lax.dynamic_slice_in_dim(branch_late, member * part_out, part_out, 1)
            return tokens_product(att_low, part).astype(BF16)

        out_came = exchange(out_columns(1 - me), "tp")
        out_term = jnp.zeros((qwidth, part_out), BF16)
        out_term = lax.dynamic_update_slice_in_dim(out_term, out_columns(me), me * heads_rows, 0)
        out_term = lax.dynamic_update_slice_in_dim(out_term, out_came, (1 - me) * heads_rows, 0)
    else:
        out_term = tokens_product(att_low, branch_late).astype(BF16)
        out_term = out_term.reshape(qwidth // n_tp, n_tp, part_out).transpose(1, 0, 2)
        out_term = group_swap(out_term).reshape(qwidth, part_out)
    half = part_out // 2
    out_parts = [out_term[:, :half], out_term[:, half:]]

    out_terms = [
        plane_stage(plane_grid(part), order[0]) for part, order in zip(out_parts, orders)
    ]
    feed_sum = after(feed_sum, in_parts[-1])
    expand_rows = ctx_swap(feed_sum[:rows_expand].reshape(n_ctx, row_in, -1))
    late = [in_terms[-1][-1]] + [terms[-1] for terms in out_terms]
    in_terms[-1][-1] = after(*late, expand_rows)
    for terms in out_terms:
        terms[-1] = after(terms[-1], late[0])
    in_terms[0][-1] = after(in_terms[0][-1], *late, expand_rows)
    expand_sum = expand_rows.reshape(n_ctx, row_in, 2, n_dp, row_down)
    expand_sum = expand_sum.transpose(1, 2, 3, 0, 4).reshape(row_in, 2 * FF).astype(F32)
    in_terms = [plane_stage(terms, order[1]) for terms, order in zip(in_terms, orders)]
    out_terms = [plane_stage(terms, order[1]) for terms, order in zip(out_terms, orders)]
    joined_all = after(jnp.concatenate(joined_parts, axis=1), in_parts[-1])
    first_part = against(joined_all, in_low).astype(BF16)

    ready = (first_part,) + tuple(terms[-1] for terms in in_terms)
    low = F32 if n_tp != 2 else BF16

    rows = column_sum(in_terms + out_terms).reshape(n_tp, row_in, -1)
    rows = group_swap(rows.astype(low)).astype(F32).transpose(1, 0, 2)
    in_sum = rows[:, :, :part_in].reshape(row_in, joined_width)
    out_sum = rows[:, :, part_in:].reshape(row_in, width)
    contract_sum = unpacked_rows(feed_sum[rows_expand:].astype(F32), row_down, width)

    inv_one = lax.rsqrt(jnp.mean(resid * resid, axis=-1, keepdims=True) + EPSILON)
    first_grad = own_sum(first_part)
    first_grad = after(first_grad, *ready[1:])
    resid_grad = hidden_grad + norm_back(first_grad, resid * inv_one, inv_one, gain_one)
    shape = (batches, rows_local, width)
    grad_inputs = from_streams(resid_grad.astype(BF16).reshape(shape))

    in_sum = from_groups(in_sum)
    low_gains = gains.astype(BF16).astype(F32)
    gain_sum = jnp.stack(
        [
            jnp.sum(in_sum * attend_in.astype(BF16).astype(F32), axis=1),
            jnp.sum(expand_sum * expand.astype(BF16).astype(F32), axis=1),
        ]
    ) / low_gains

    out_fan = max(1, HEADS * HEAD_DIM // (stream // 8))
    new_in = adamw(attend_in, attend_in_first, attend_in_second, in_sum, RATE / math.sqrt(D))
    new_out = adamw(
        attend_out, attend_out_first, attend_out_second, out_sum, RATE / math.sqrt(out_fan)
    )
    new_gain = adamw(gains, gains_first, gains_second, gain_sum, GAIN_RATE)
    new_expand = adamw(expand, expand_first, expand_second, expand_sum, RATE / math.sqrt(D))
    new_contract = adamw(
        contract, contract_first, contract_second, contract_sum, RATE / math.sqrt(FF)
    )
    return (block_out, grad_inputs, *new_in, *new_out, *new_gain, *new_expand, *new_contract)


def solution(mesh):
    n_dp, n_ctx = mesh.shape["dp"], mesh.shape["ctx"]
    cut = jax.sharding.Mesh(
        mesh.devices.reshape(n_dp, 2, 2, n_ctx // 4), ("dp", "hi", "lo", "tp")
    )
    every = ("dp", "hi", "lo", "tp")
    rows = P(every, None)
    columns = P(None, every)
    tokens = P(None, every, None)
    return jax.shard_map(
        local,
        mesh=cut,
        in_specs=(tokens, columns, tokens, rows, rows, columns, rows, rows)
        + (rows,) * 4
        + (columns,) * 2
        + (rows,) * 4,
        out_specs=(tokens, tokens) + (rows,) * 6 + (columns,) * 3 + (rows,) * 6,
        check_vma=False,
    )
```
